32 devices in a mesh: slab: 8 (over y, x, core), angle: 4 (over z).
Axes of the slice: x: 2, y: 2, z: 4, core: 2. Of those that a mesh axis runs over, the one named last changes fastest.
Arguments:
- projector: bfloat16 [4096, 128, 128], P(('slab', 'angle')), may hold values from 0 to 2, as said below
- block_vox: int32 [4096], P(('slab', 'angle')), may hold values from 0 to 63
- block_slot: int32 [4096], P(('slab', 'angle')), may hold values from 0 to 191, as said below
- send_ray: int32 [32, 192], P(('slab', 'angle')), may hold values from 0 to 31, as said below
- block_count: int32 [32], P(('slab', 'angle')), may hold values from 24 to 128, as said below
- prior: float32 [512, 128], P('slab'), may hold values from -6 to 6
- sinogram: float32 [1024, 128], P(('slab', 'angle')), may hold values from -12 to 12
Outputs:
- volume: float32 [512, 128], P('slab')
- residual: float32 [1024, 128], P(('slab', 'angle'))
The draws below stay inside these ranges and needn't reach their ends.
Inputs may be any that keep to these rules, and one draw needn't show every extreme that they name: `block_slot`: entry k names a send slot o * 24 + j with j < 24, where o is the slab index that owns the rays of block k in the block's angle group. `send_ray`: within a row, the 24 entries of each owner's slots are distinct. Slots that no stored block names carry an arbitrary ray block. `block_count`: some device stores all 128 slots. `projector`: entries are nonnegative.
All inputs are finite; a program needn't handle non-finite values.
Results may differ from the reference program's by a relative error of at most 0.00076.
Values may be sent and summed in bfloat16 or wider, within the bound.
No kernel may reach another device: no remote copies, remote signals or barrier semaphores. Data moves between devices by JAX's collectives and lax.ppermute only.
A program may use at most 64 MiB of HBM per device.

```python
import math
import jax
import jax.numpy as jnp
from jax import lax

BLK = 128
VB_DEV = 64
ITERS = 2
RB_DEV = 32
NNZ_DEV = 128
CAP = 24
VB_TOT = 512
RAY_ROWS = 1024
NNZ_TOT = 4096
N_SLAB = 8
N_ANGLE = 4


def draw_projector(key, part):
    key_off = jax.random.fold_in(key, 101)
    key_row = jax.random.fold_in(key, 102)
    key_col = jax.random.fold_in(key, 103)
    key_diag = jax.random.fold_in(key, 104)
    spread = jax.random.uniform(key_off, (NNZ_TOT, BLK, BLK), jnp.float32)
    row_scale = jnp.exp(jax.random.uniform(key_row, (NNZ_TOT, BLK, 1), jnp.float32) * math.log(10.0))
    col_scale = jnp.exp(jax.random.uniform(key_col, (NNZ_TOT, 1, BLK), jnp.float32) * math.log(10.0))
    diagonal = jax.random.uniform(key_diag, (NNZ_TOT, BLK, 1), jnp.float32, 0.5, 1.5)
    offdiag = 0.0015 * spread * row_scale * col_scale
    on_diag = lax.broadcasted_iota(jnp.int32, (BLK, BLK), 0) == lax.broadcasted_iota(jnp.int32, (BLK, BLK), 1)
    return jnp.where(on_diag[None, :, :], diagonal, offdiag).astype(jnp.bfloat16)


def draw_block_slot(key, part):
    device_total = N_SLAB * N_ANGLE
    key_full = jax.random.fold_in(key, 201)
    key_owner = jax.random.fold_in(key, 202)
    key_within = jax.random.fold_in(key, 203)
    full_owner = jax.random.randint(key_full, (N_ANGLE,), 0, N_SLAB, dtype=jnp.int32)
    owners = jax.random.randint(key_owner, (device_total, NNZ_DEV), 0, N_SLAB, dtype=jnp.int32)
    within = jax.random.randint(key_within, (device_total, NNZ_DEV), 0, CAP, dtype=jnp.int32)
    position = jnp.arange(NNZ_DEV, dtype=jnp.int32)[None, :]
    group_of = (jnp.arange(device_total, dtype=jnp.int32) % N_ANGLE)[:, None]
    forced = position < CAP
    owners = jnp.where(forced, full_owner[group_of], owners)
    within = jnp.where(forced, position, within)
    return (owners * CAP + within).reshape(-1).astype(jnp.int32)


def draw_send_ray(key, part):
    device_total = N_SLAB * N_ANGLE
    key_score = jax.random.fold_in(key, 301)
    scores = jax.random.randint(key_score, (device_total, N_SLAB, RB_DEV), 0, 65536, dtype=jnp.int32)
    scores = scores * RB_DEV + jnp.arange(RB_DEV, dtype=jnp.int32)[None, None, :]
    picked = jnp.argsort(scores, axis=-1)[:, :, :CAP]
    return picked.reshape(device_total, N_SLAB * CAP).astype(jnp.int32)


def draw_block_count(key, part):
    device_total = N_SLAB * N_ANGLE
    key_count = jax.random.fold_in(key, 401)
    key_pick = jax.random.fold_in(key, 402)
    counts = jax.random.randint(key_count, (device_total,), CAP, NNZ_DEV + 1, dtype=jnp.int32)
    busiest = jax.random.randint(key_pick, (), 0, device_total, dtype=jnp.int32)
    return jnp.where(jnp.arange(device_total, dtype=jnp.int32) == busiest, NNZ_DEV, counts).astype(jnp.int32)


def set_ends(drawn, key, low, top_value):
    longest = drawn.shape.index(max(drawn.shape))
    spots = []
    for shift in (0, 1):
        where = [jax.random.randint(jax.random.fold_in(key, axis), (), 0, length) for axis, length in enumerate(drawn.shape)]
        where[longest] = (where[longest] + shift) % drawn.shape[longest]
        spots.append(tuple(where))
    return drawn.at[spots[0]].set(low).at[spots[1]].set(top_value)


def levels(rng, shape, shards, least, high):
    def one(dim, blocks):
        draws = jax.random.uniform(jax.random.fold_in(jax.random.fold_in(rng, 6), dim), (blocks,), jnp.float32, least / len(shards), high / len(shards))
        return jnp.repeat(jnp.exp(draws), shape[dim] // blocks).reshape((-1,) + (1,) * (len(shape) - dim - 1))

    factor_of = one(*shards[0])
    for cut in shards[1:]:
        factor_of = factor_of * one(*cut)
    return factor_of


def normal_values(stream_key, shape, scale, reach, shards=(), kind=jnp.bfloat16):
    gain = levels(stream_key, shape, shards, -0.22, 0.18) if shards else 1.0
    array = jax.random.normal(stream_key, shape, jnp.float32) * scale * gain
    return jnp.minimum(jnp.maximum(array, -reach), reach).astype(kind)


def setup_inputs(seed: int = 0) -> dict:
    key_list = jax.random.split(jax.random.key(seed), 8)
    projector = draw_projector(jax.random.fold_in(key_list[7], 71), 0)
    block_vox = set_ends(jax.random.randint(key_list[1], (NNZ_TOT,), 0, VB_DEV), jax.random.fold_in(key_list[1], 1), 0, VB_DEV - 1).astype(jnp.int32)
    block_slot = draw_block_slot(jax.random.fold_in(key_list[7], 71), 0)
    send_ray = draw_send_ray(jax.random.fold_in(key_list[7], 71), 0)
    block_count = draw_block_count(jax.random.fold_in(key_list[7], 71), 0)
    prior = normal_values(key_list[5], (VB_TOT, BLK), 1.0, 6.0, ((0, 8),), jnp.float32)
    sinogram = normal_values(key_list[6], (RAY_ROWS, BLK), 2.0, 12.0, ((0, 32),), jnp.float32)
    return {"projector": projector, "block_vox": block_vox, "block_slot": block_slot, "send_ray": send_ray, "block_count": block_count, "prior": prior, "sinogram": sinogram}


def reference(projector, block_vox, block_slot, send_ray, block_count, prior, sinogram):
    device_total = N_SLAB * N_ANGLE
    tiles = projector.reshape(device_total, NNZ_DEV, BLK, BLK)
    device_ids = jnp.arange(device_total, dtype=jnp.int32)
    slab_of = device_ids // N_ANGLE
    group_of = device_ids % N_ANGLE
    slot_of = block_slot.reshape(device_total, NNZ_DEV).astype(jnp.int32)
    owners = slot_of // CAP
    local_ray = jnp.take_along_axis(send_ray, slot_of, axis=1).astype(jnp.int32)
    ray_rows = ((owners * N_ANGLE + group_of[:, None]) * RB_DEV + local_ray).astype(jnp.int32)
    vox_rows = (slab_of[:, None] * VB_DEV + block_vox.reshape(device_total, NNZ_DEV)).astype(jnp.int32)
    usable = (jnp.arange(NNZ_DEV, dtype=jnp.int32)[None, :] < block_count[:, None]).astype(jnp.float32)
    items = (tiles, ray_rows, vox_rows, usable)
    highest = lax.Precision.HIGHEST

    def row_sums():
        def accumulate(total, item):
            tile, rows_in, vox_in, mask = item
            terms = jnp.sum(tile.astype(jnp.float32), axis=2)
            return total.at[rows_in].add(terms * mask[:, None]), None
        total, _ = lax.scan(accumulate, jnp.zeros((RAY_ROWS, BLK), jnp.float32), items)
        return total

    def col_sums():
        def accumulate(total, item):
            tile, rows_in, vox_in, mask = item
            terms = jnp.sum(tile.astype(jnp.float32), axis=1)
            return total.at[vox_in].add(terms * mask[:, None]), None
        total, _ = lax.scan(accumulate, jnp.zeros((VB_TOT, BLK), jnp.float32), items)
        return total

    def forward(volume_bf):
        def accumulate(total, item):
            tile, rows_in, vox_in, mask = item
            inputs = volume_bf[vox_in].astype(jnp.float32)
            terms = jnp.einsum("kij,kj->ki", tile.astype(jnp.float32), inputs, precision=highest)
            return total.at[rows_in].add(terms * mask[:, None]), None
        total, _ = lax.scan(accumulate, jnp.zeros((RAY_ROWS, BLK), jnp.float32), items)
        return total

    def backward(residual_bf):
        def accumulate(total, item):
            tile, rows_in, vox_in, mask = item
            picked = residual_bf[rows_in].astype(jnp.float32)
            terms = jnp.einsum("kij,ki->kj", tile.astype(jnp.float32), picked, precision=highest)
            return total.at[vox_in].add(terms * mask[:, None]), None
        total, _ = lax.scan(accumulate, jnp.zeros((VB_TOT, BLK), jnp.float32), items)
        return total

    row_weight = 1.0 / jnp.maximum(row_sums(), 1.0)
    col_weight = 1.0 / jnp.maximum(col_sums(), 1.0)
    volume = prior
    residual = jnp.zeros((RAY_ROWS, BLK), jnp.float32)
    for iteration in range(ITERS):
        projected = forward(volume.astype(jnp.bfloat16))
        residual = row_weight * (sinogram - projected)
        correction = backward(residual.astype(jnp.bfloat16))
        volume = volume + col_weight * correction
    return volume, residual
```

```python
import jax
import jax.numpy as jnp
from jax import lax
from jax.experimental import pallas as pl
from jax.experimental.pallas import tpu as pltpu
from jax.sharding import PartitionSpec as P

ITERS = 2
F32 = jnp.float32
BF16 = jnp.bfloat16
BLK = 128
CHUNKS = 8


def whole(space=pltpu.VMEM):
    return pl.BlockSpec(memory_space=space)


def iota(shape, dim):
    return lax.broadcasted_iota(jnp.int32, shape, dim)


def split3(x):
    hi = x.astype(BF16)
    rest = x - hi.astype(F32)
    mid = rest.astype(BF16)
    low = (rest - mid.astype(F32)).astype(BF16)
    return hi, mid, low


def dot(a, b, dims=((1,), (0,))):
    return lax.dot_general(a, b, (dims, ((), ())), preferred_element_type=F32)


def one_hot_t(row, size):
    return jnp.where(iota((size, row.shape[1]), 0) == row, 1.0, 0.0)


def block_rows(slot_ref, ray_ref, count_ref, slabs, capacity, ray_dev):
    slot = slot_ref[...]
    slots = ray_ref.shape[1]
    picks = one_hot_t(slot, slots).astype(BF16)
    rays = jnp.broadcast_to(ray_ref[...], (16, slots)).astype(F32).astype(BF16)
    ray = dot(rays, picks)[0:1, :].astype(jnp.int32)
    owner = jnp.zeros_like(slot)
    for o in range(1, slabs):
        owner = owner + jnp.where(slot >= o * capacity, 1, 0)
    stored = iota(slot.shape, 1) < count_ref[0]
    return jnp.where(stored, owner * ray_dev + ray, -1)


def forward(proj, volume, vox, sums, before=None):
    blocks = proj.shape[0]
    half = blocks // 2
    picked = dot(volume.T.astype(BF16), one_hot_t(vox, volume.shape[0]).astype(BF16))
    lane = iota((BLK, blocks), 1)
    weights = jnp.concatenate([jnp.where(lane < half, picked, 0.0), jnp.where(lane >= half, picked, 0.0)], 0)
    if sums:
        ones = jnp.concatenate([jnp.where(lane < half, 1.0, 0.0), jnp.where(lane >= half, 1.0, 0.0)], 0)
        weights = jnp.concatenate([weights, ones], 1)
    weights = weights.astype(BF16)
    width = weights.shape[1]
    column = lax.rem(iota((BLK, width), 1), half)

    def step(p, acc):
        pair = jnp.concatenate([proj[p], proj[p + half]], 1)
        return jnp.where(column == p, dot(pair, weights), acc)

    acc = jnp.zeros((BLK, width), F32)
    per = half // CHUNKS
    for c in range(CHUNKS):
        if before is not None:
            before(c)
        for p in range(c * per, (c + 1) * per):
            acc = step(p, acc)
    return acc


def spread(rows, columns, total):
    spots = one_hot_t(rows, total).astype(BF16)
    out = None
    for term in split3(columns):
        part = dot(spots, term, ((1,), (1,)))
        out = part if out is None else out + part
    return out


def backward(proj, weighted, rows, vox, vox_dev, sums):
    blocks = proj.shape[0]
    spots = one_hot_t(rows, weighted.shape[0])
    picked = dot(spots.T.astype(BF16), weighted.astype(BF16)).astype(BF16)
    group = 16
    row = iota((group, BLK), 0)
    stored = jnp.where(rows >= 0, 1.0, 0.0)
    places = (one_hot_t(vox, vox_dev) * stored).astype(BF16)
    tops, lows = [], []
    for g in range(blocks // group):
        mine = picked[g * group:(g + 1) * group].astype(F32)
        left = [jnp.where(row == c, mine, 0.0) for c in range(group)]
        left = jnp.concatenate(left, 1)
        if sums:
            ones = jnp.concatenate([jnp.where(row == c, 1.0, 0.0) for c in range(group)], 1)
            left = jnp.concatenate([left, ones], 0)
        right = proj[g * group:(g + 1) * group].reshape(group * BLK, BLK)
        out = dot(left.astype(BF16), right)
        tops.append(out[:group])
        if sums:
            lows.append(out[group:])
    columns = jnp.concatenate(tops, 0)
    if sums:
        columns = jnp.concatenate([columns, jnp.concatenate(lows, 0)], 1)
    out = None
    for term in split3(columns):
        part = dot(places, term)
        out = part if out is None else out + part
    return out


def place_own(out_ref, sino_ref, ray_dev, start):
    me = lax.axis_index("slab")
    at = pl.ds(pl.multiple_of(start + me * ray_dev, 8), ray_dev)
    out_ref[at, :] = out_ref[at, :] + sino_ref[...]


def first_forward(slabs, capacity, ray_dev):
    def kernel(count, proj_hbm, vox, slot, ray, prior, sino, proj, rows_out, part, sems):
        blocks = proj_hbm.shape[0]
        half = blocks // 2
        per = half // CHUNKS
        copies = []
        for c in range(CHUNKS):
            for h in range(2):
                at = pl.ds(h * half + c * per, per)
                copy = pltpu.make_async_copy(proj_hbm.at[at], proj.at[at], sems.at[2 * c + h])
                copy.start()
                copies.append(copy)

        def before(c):
            copies[2 * c].wait()
            copies[2 * c + 1].wait()

        rows = block_rows(slot, ray, count, slabs, capacity, ray_dev)
        rows_out[...] = rows
        total = slabs * ray_dev
        columns = forward(proj, prior[...], vox[...], True, before)
        part[0:total, :] = -spread(rows, columns[:, :blocks], total)
        part[total:2 * total, :] = spread(rows, columns[:, blocks:], total)
        place_own(part, sino, ray_dev, 0)

    return kernel


def first_backward(ray_dev):
    def kernel(proj, rows, vox, own, other, weight, corr):
        total = own.shape[0] // 2
        sums = own[...] + other[...]
        weights = 1.0 / jnp.maximum(sums[total:], 1.0)
        weight[...] = weights
        both = backward(proj, weights * sums[:total], rows[...], vox[...], corr.shape[0] // 2, True)
        vox_dev = corr.shape[0] // 2
        corr[0:vox_dev, :] = both[:, :BLK]
        corr[vox_dev:2 * vox_dev, :] = both[:, BLK:]

    return kernel


def next_forward(ray_dev):
    def kernel(proj, rows, vox, volume, corr, sino, volume_out, weight_out, part):
        vox_dev = volume.shape[0]
        weights = 1.0 / jnp.maximum(corr[vox_dev:2 * vox_dev, :], 1.0)
        weight_out[...] = weights
        updated = volume[...] + weights * corr[0:vox_dev, :]
        volume_out[...] = updated
        columns = forward(proj, updated, vox[...], False)
        part[...] = -spread(rows[...], columns, part.shape[0])
        place_own(part, sino, ray_dev, 0)

    return kernel


def last_backward(ray_dev):
    def kernel(proj, rows, vox, own, other, weight, residual, corr):
        weighted = weight[...] * (own[...] + other[...])
        corr[...] = backward(proj, weighted, rows[...], vox[...], corr.shape[0], False)
        me = lax.axis_index("slab")
        residual[...] = weight[pl.ds(pl.multiple_of(me * ray_dev, 8), ray_dev), :] * (
            own[pl.ds(pl.multiple_of(me * ray_dev, 8), ray_dev), :]
            + other[pl.ds(pl.multiple_of(me * ray_dev, 8), ray_dev), :]
        )

    return kernel


def swap(x, axis, bit):
    size = lax.axis_size(axis)
    return lax.ppermute(x, axis, [(i, i ^ bit) for i in range(size)])


def over_slabs(x):
    slabs = lax.axis_size("slab")
    x, other = x, swap(x, "slab", 1)
    bits = [1 << b for b in range(1, slabs.bit_length() - 1)]
    while bits:
        x = x + other
        if len(bits) == 1:
            x, other, bits = x, swap(x, "slab", bits[0]), []
            continue
        first, second, bits = bits[0], bits[1], bits[2:]
        rows = x.shape[0] // 2
        core = lax.rem(lax.axis_index("slab"), 2)
        half = lax.dynamic_slice_in_dim(x, core * rows, rows)
        near = lax.ppermute(x, "slab", [(i, i ^ (second if i & 1 else first)) for i in range(slabs)])
        far = swap(half, "slab", first | second)
        got = lax.dynamic_update_slice_in_dim(
            near, lax.dynamic_slice_in_dim(near, core * rows, rows) + far, core * rows, 0
        )
        x, other = x + got, swap(got, "slab", 1)
    return x, other


def over_angles(x):
    slabs, angles = lax.axis_size("slab"), lax.axis_size("angle")
    bits = [1 << b for b in range(angles.bit_length() - 1)]
    core = lax.rem(lax.axis_index("slab"), 2)
    while bits:
        if len(bits) == 1:
            x, bits = x + swap(x, "angle", bits[0]), []
            continue
        first, second, bits = bits[0], bits[1], bits[2:]
        other = swap(x, "slab", 1)
        both = jnp.stack([jnp.where(core == 0, x, other), jnp.where(core == 0, other, x)])
        pairs = [
            (s * angles + g, s * angles + (g ^ (second if s & 1 else first)))
            for s in range(slabs)
            for g in range(angles)
        ]
        near = lax.ppermute(both, ("slab", "angle"), pairs)
        far = swap(x, "angle", first | second)
        mine = lax.dynamic_index_in_dim(near, core, 0, keepdims=False)
        theirs = swap(lax.dynamic_index_in_dim(near, 1 - core, 0, keepdims=False), "slab", 1)
        by_first = jnp.where(core == 0, mine, theirs)
        by_second = jnp.where(core == 0, theirs, mine)
        x = (x + by_first) + (by_second + far)
    return x


def local(projector, block_vox, block_slot, send_ray, block_count, prior, sinogram):
    slabs = lax.axis_size("slab")
    capacity = send_ray.shape[1] // slabs
    ray_dev = sinogram.shape[0]
    vox_dev = prior.shape[0]
    blocks = projector.shape[0]
    total = slabs * ray_dev
    params = pltpu.CompilerParams(vmem_limit_bytes=40 * 1024 * 1024)
    vmem = lambda rows, dtype=F32: pltpu.VMEM((rows, BLK), dtype)
    vox = block_vox.reshape(1, blocks)
    slot = block_slot.reshape(1, blocks)

    proj, rows, part = pl.pallas_call(
        first_forward(slabs, capacity, ray_dev),
        out_shape=(
            pltpu.VMEM(projector.shape, BF16),
            pltpu.VMEM((1, blocks), jnp.int32),
            vmem(2 * total),
        ),
        in_specs=[whole(pltpu.SMEM), whole(pl.ANY)] + [whole()] * 5,
        out_specs=(whole(), whole(), whole()),
        scratch_shapes=[pltpu.SemaphoreType.DMA((2 * CHUNKS,))],
        compiler_params=params,
        name="first_forward",
    )(block_count, projector, vox, slot, send_ray, prior, sinogram)
    own, other = over_slabs(part)

    row_weight, corr = pl.pallas_call(
        first_backward(ray_dev),
        out_shape=(vmem(total), vmem(2 * vox_dev)),
        in_specs=[whole()] * 5,
        out_specs=(whole(), whole()),
        compiler_params=params,
        name="first_backward",
    )(proj, rows, vox, own, other)
    corr = over_angles(corr)

    volume, col_weight, part = pl.pallas_call(
        next_forward(ray_dev),
        out_shape=(vmem(vox_dev), vmem(vox_dev), vmem(total)),
        in_specs=[whole()] * 6,
        out_specs=(whole(),) * 3,
        compiler_params=params,
        name="next_forward",
    )(proj, rows, vox, prior, corr, sinogram)
    own, other = over_slabs(part)

    residual, corr = pl.pallas_call(
        last_backward(ray_dev),
        out_shape=(jax.ShapeDtypeStruct((ray_dev, BLK), F32), vmem(vox_dev)),
        in_specs=[whole()] * 6,
        out_specs=(whole(), whole()),
        compiler_params=params,
        name="last_backward",
    )(proj, rows, vox, own, other, row_weight)
    corr = over_angles(corr)
    return volume + col_weight * corr, residual


def solution(mesh):
    return jax.shard_map(
        local,
        mesh=mesh,
        in_specs=(
            P(("slab", "angle"), None, None),
            P(("slab", "angle")),
            P(("slab", "angle")),
            P(("slab", "angle"), None),
            P(("slab", "angle")),
            P("slab", None),
            P(("slab", "angle"), None),
        ),
        out_specs=(P("slab", None), P(("slab", "angle"), None)),
        check_vma=False,
    )
```

```python
import jax
import jax.numpy as jnp
from jax import lax
from jax.experimental import pallas as pl
from jax.experimental.pallas import tpu as pltpu
from jax.sharding import PartitionSpec as P

ITERS = 2
F32 = jnp.float32
BF16 = jnp.bfloat16
BLK = 128
CHUNKS = 8


def whole(space=pltpu.VMEM):
    return pl.BlockSpec(memory_space=space)


def iota(shape, dim):
    return lax.broadcasted_iota(jnp.int32, shape, dim)


def split3(x):
    hi = x.astype(BF16)
    rest = x - hi.astype(F32)
    mid = rest.astype(BF16)
    low = (rest - mid.astype(F32)).astype(BF16)
    return hi, mid, low


def dot(a, b, dims=((1,), (0,))):
    return lax.dot_general(a, b, (dims, ((), ())), preferred_element_type=F32)


def one_hot_t(row, size):
    return jnp.where(iota((size, row.shape[1]), 0) == row, 1.0, 0.0)


def block_rows(slot, ray, count, slabs, capacity, ray_dev):
    slots = ray.shape[1]
    picks = one_hot_t(slot, slots).astype(BF16)
    rays = jnp.broadcast_to(ray, (16, slots)).astype(F32).astype(BF16)
    ray = dot(rays, picks)[0:1, :].astype(jnp.int32)
    owner = jnp.zeros_like(slot)
    for o in range(1, slabs):
        owner = owner + jnp.where(slot >= o * capacity, 1, 0)
    place = (owner & 1) * (slabs // 2) + (owner >> 1)
    stored = iota(slot.shape, 1) < count
    return jnp.where(stored, place * ray_dev + ray, -1)


def forward(proj, volume, vox, sums, before=None):
    blocks = proj.shape[0]
    half = blocks // 2
    picked = dot(volume.T.astype(BF16), one_hot_t(vox, volume.shape[0]).astype(BF16))
    lane = iota((BLK, blocks), 1)
    weights = jnp.concatenate([jnp.where(lane < half, picked, 0.0), jnp.where(lane >= half, picked, 0.0)], 0)
    if sums:
        ones = jnp.concatenate([jnp.where(lane < half, 1.0, 0.0), jnp.where(lane >= half, 1.0, 0.0)], 0)
        weights = jnp.concatenate([weights, ones], 1)
    weights = weights.astype(BF16)
    width = weights.shape[1]
    column = lax.rem(iota((BLK, width), 1), half)

    def step(p, acc):
        pair = jnp.concatenate([proj[p], proj[p + half]], 1)
        return jnp.where(column == p, dot(pair, weights), acc)

    acc = jnp.zeros((BLK, width), F32)
    per = half // CHUNKS
    for c in range(CHUNKS):
        if before is not None:
            before(c)
        for p in range(c * per, (c + 1) * per):
            acc = step(p, acc)
    return acc


def spread(rows, columns, total):
    spots = one_hot_t(rows, total).astype(BF16)
    out = None
    for term in split3(columns):
        part = dot(spots, term, ((1,), (1,)))
        out = part if out is None else out + part
    return out


def backward(proj, weighted, rows, vox, vox_dev, sums):
    blocks = proj.shape[0]
    spots = one_hot_t(rows, weighted.shape[0])
    picked = dot(spots.T.astype(BF16), weighted.astype(BF16)).astype(BF16)
    group = 16
    row = iota((group, BLK), 0)
    stored = jnp.where(rows >= 0, 1.0, 0.0)
    places = (one_hot_t(vox, vox_dev) * stored).astype(BF16)
    tops, lows = [], []
    for g in range(blocks // group):
        mine = picked[g * group:(g + 1) * group].astype(F32)
        left = [jnp.where(row == c, mine, 0.0) for c in range(group)]
        left = jnp.concatenate(left, 1)
        if sums:
            ones = jnp.concatenate([jnp.where(row == c, 1.0, 0.0) for c in range(group)], 1)
            left = jnp.concatenate([left, ones], 0)
        right = proj[g * group:(g + 1) * group].reshape(group * BLK, BLK)
        out = dot(left.astype(BF16), right)
        tops.append(out[:group])
        if sums:
            lows.append(out[group:])
    columns = jnp.concatenate(tops, 0)
    if sums:
        columns = jnp.concatenate([columns, jnp.concatenate(lows, 0)], 1)
    out = None
    for term in split3(columns):
        part = dot(places, term)
        out = part if out is None else out + part
    return out


def put_partial(sums, sino, mine, theirs, ray_dev):
    half = sums.shape[0] // 2
    slab = lax.axis_index("slab")
    core = lax.rem(slab, 2)
    top, low = sums[:half], sums[half:]
    mine[0:half, :] = -jnp.where(core == 0, top, low)
    theirs[0:half, :] = -jnp.where(core == 0, low, top)
    at = pl.ds(pl.multiple_of((slab >> 1) * ray_dev, 8), ray_dev)
    mine[at, :] = mine[at, :] + sino


def first_forward(slabs, capacity, ray_dev):
    def kernel(proj_hbm, vox_hbm, slot_hbm, ray_hbm, count_hbm, prior_hbm, sino_hbm,
               proj, vox, rows_out, prior, sino, mine, theirs, slot, ray, count, sems, small):
        blocks = proj_hbm.shape[0]
        half = blocks // 2
        per = half // CHUNKS
        smalls = [
            pltpu.make_async_copy(source, target, small.at[i])
            for i, (source, target) in enumerate([
                (vox_hbm, vox), (slot_hbm, slot), (ray_hbm, ray), (count_hbm, count),
                (prior_hbm, prior), (sino_hbm, sino),
            ])
        ]
        for copy in smalls:
            copy.start()
        copies = []
        for c in range(CHUNKS):
            for h in range(2):
                at = pl.ds(h * half + c * per, per)
                copy = pltpu.make_async_copy(proj_hbm.at[at], proj.at[at], sems.at[2 * c + h])
                copy.start()
                copies.append(copy)
        for copy in smalls:
            copy.wait()

        def before(c):
            copies[2 * c].wait()
            copies[2 * c + 1].wait()

        rows = block_rows(slot[...], ray[...], count[...], slabs, capacity, ray_dev)
        rows_out[...] = rows
        total = slabs * ray_dev
        columns = forward(proj, prior[...], vox[...], True, before)
        put_partial(spread(rows, columns[:, :blocks], total), sino[...], mine, theirs, ray_dev)
        sums = spread(rows, columns[:, blocks:], total)
        core = lax.rem(lax.axis_index("slab"), 2)
        top, low = sums[:total // 2], sums[total // 2:]
        mine[total // 2:total, :] = jnp.where(core == 0, top, low)
        theirs[total // 2:total, :] = jnp.where(core == 0, low, top)

    return kernel


def join_halves(mine, theirs):
    core = lax.rem(lax.axis_index("slab"), 2)
    mine, theirs = mine[...], theirs[...]
    return jnp.concatenate([jnp.where(core == 0, mine, theirs), jnp.where(core == 0, theirs, mine)], 0)


def first_backward(proj, rows, vox, mine, theirs, corr):
    vox_dev = corr.shape[0] // 2
    both = backward(proj, join_halves(mine, theirs), rows[...], vox[...], vox_dev, True)
    corr[0:vox_dev, :] = both[:, :BLK]
    corr[vox_dev:2 * vox_dev, :] = both[:, BLK:]


def next_forward(ray_dev):
    def kernel(proj, rows, vox, volume, corr, sino, volume_out, weight_out, mine, theirs):
        vox_dev = volume.shape[0]
        weights = 1.0 / jnp.maximum(corr[vox_dev:2 * vox_dev, :], 1.0)
        weight_out[...] = weights
        updated = volume[...] + weights * corr[0:vox_dev, :]
        volume_out[...] = updated
        columns = forward(proj, updated, vox[...], False)
        put_partial(spread(rows[...], columns, 2 * mine.shape[0]), sino[...], mine, theirs, ray_dev)

    return kernel


def last_backward(proj, rows, vox, mine, theirs, corr):
    corr[...] = backward(proj, join_halves(mine, theirs), rows[...], vox[...], corr.shape[0], False)


def swap(x, axis, bit):
    size = lax.axis_size(axis)
    return lax.ppermute(x, axis, [(i, i ^ bit) for i in range(size)])


def over_slabs(mine, theirs):
    slabs = lax.axis_size("slab")
    x = mine + swap(theirs, "slab", 1)
    bits = [1 << b for b in range(1, slabs.bit_length() - 1)]
    while bits:
        if len(bits) == 1:
            x, bits = x + swap(x, "slab", bits[0]), []
            continue
        first, second, bits = bits[0], bits[1], bits[2:]
        x = (x + swap(x, "slab", first)) + (swap(x, "slab", second) + swap(x, "slab", first | second))
    return x


def over_angles(x):
    slabs, angles = lax.axis_size("slab"), lax.axis_size("angle")
    bits = [1 << b for b in range(angles.bit_length() - 1)]
    for bit in bits:
        x = x + swap(x, "angle", bit)
    return x


def local(projector, block_vox, block_slot, send_ray, block_count, prior, sinogram):
    slabs = lax.axis_size("slab")
    capacity = send_ray.shape[1] // slabs
    ray_dev = sinogram.shape[0]
    vox_dev = prior.shape[0]
    blocks = projector.shape[0]
    half = slabs * ray_dev // 2
    params = pltpu.CompilerParams(vmem_limit_bytes=8 * 1024 * 1024)
    vmem = lambda rows, dtype=F32: pltpu.VMEM((rows, BLK), dtype)
    line = pltpu.VMEM((1, blocks), jnp.int32)
    arguments = (
        projector, block_vox.reshape(1, blocks), block_slot.reshape(1, blocks), send_ray,
        block_count.reshape(1, 1), prior, sinogram,
    )

    proj, vox, rows, volume, sino, mine, theirs = pl.pallas_call(
        first_forward(slabs, capacity, ray_dev),
        out_shape=(
            pltpu.VMEM(projector.shape, BF16), line, line, vmem(vox_dev), vmem(ray_dev),
            vmem(2 * half), vmem(2 * half),
        ),
        in_specs=[whole(pl.ANY)] * 7,
        out_specs=(whole(),) * 7,
        scratch_shapes=[
            line,
            pltpu.VMEM(send_ray.shape, jnp.int32),
            pltpu.VMEM((1, 1), jnp.int32),
            pltpu.SemaphoreType.DMA((2 * CHUNKS,)),
            pltpu.SemaphoreType.DMA((6,)),
        ],
        compiler_params=params,
        name="first_forward",
    )(*[x if x.size == 1 else pltpu.with_memory_space_constraint(x, pltpu.HBM) for x in arguments])
    sums = over_slabs(mine, theirs)
    row_weight = 1.0 / jnp.maximum(sums[half:], 1.0)
    weighted = (row_weight * sums[:half]).astype(BF16)

    corr = pl.pallas_call(
        first_backward,
        out_shape=vmem(2 * vox_dev),
        in_specs=[whole()] * 5,
        out_specs=whole(),
        compiler_params=params,
        name="first_backward",
    )(proj, rows, vox, weighted, swap(weighted, "slab", 1))
    corr = over_angles(corr)

    volume, col_weight, mine, theirs = pl.pallas_call(
        next_forward(ray_dev),
        out_shape=(vmem(vox_dev), vmem(vox_dev), vmem(half), vmem(half)),
        in_specs=[whole()] * 6,
        out_specs=(whole(),) * 4,
        compiler_params=params,
        name="next_forward",
    )(proj, rows, vox, volume, corr, sino)
    residual = row_weight * over_slabs(mine, theirs)
    weighted = residual.astype(BF16)
    start = lax.div(lax.axis_index("slab"), 2) * ray_dev
    residual = lax.dynamic_slice_in_dim(residual, start, ray_dev)

    corr = pl.pallas_call(
        last_backward,
        out_shape=vmem(vox_dev),
        in_specs=[whole()] * 5,
        out_specs=whole(),
        compiler_params=params,
        name="last_backward",
    )(proj, rows, vox, weighted, swap(weighted, "slab", 1))
    corr = over_angles(corr)
    return volume + col_weight * corr, residual


def solution(mesh):
    return jax.shard_map(
        local,
        mesh=mesh,
        in_specs=(
            P(("slab", "angle"), None, None),
            P(("slab", "angle")),
            P(("slab", "angle")),
            P(("slab", "angle"), None),
            P(("slab", "angle")),
            P("slab", None),
            P(("slab", "angle"), None),
        ),
        out_specs=(P("slab", None), P(("slab", "angle"), None)),
        check_vma=False,
    )
```

```python
import jax
import jax.numpy as jnp
from jax import lax
from jax.experimental import pallas as pl
from jax.experimental.pallas import tpu as pltpu
from jax.sharding import PartitionSpec as P

ITERS = 2
F32 = jnp.float32
BF16 = jnp.bfloat16
BLK = 128
CHUNKS = 2


def whole(space=pltpu.VMEM):
    return pl.BlockSpec(memory_space=space)


def iota(shape, dim):
    return lax.broadcasted_iota(jnp.int32, shape, dim)


def split3(x):
    hi = x.astype(BF16)
    rest = x - hi.astype(F32)
    mid = rest.astype(BF16)
    low = (rest - mid.astype(F32)).astype(BF16)
    return hi, mid, low


def dot(a, b, dims=((1,), (0,))):
    return lax.dot_general(a, b, (dims, ((), ())), preferred_element_type=F32)


def one_hot_t(row, size):
    return jnp.where(iota((size, row.shape[1]), 0) == row, 1.0, 0.0)


def block_rows(slot, ray, count, slabs, capacity, ray_dev):
    slots = ray.shape[1]
    picks = one_hot_t(slot, slots).astype(BF16)
    rays = jnp.broadcast_to(ray, (16, slots)).astype(F32).astype(BF16)
    ray = dot(rays, picks)[0:1, :].astype(jnp.int32)
    owner = jnp.zeros_like(slot)
    for o in range(1, slabs):
        owner = owner + jnp.where(slot >= o * capacity, 1, 0)
    place = (owner & 1) * (slabs // 2) + (owner >> 1)
    stored = iota(slot.shape, 1) < count
    return jnp.where(stored, place * ray_dev + ray, -1)


def forward(proj, volume, vox, sums, before=None):
    blocks = proj.shape[0]
    half = blocks // 2
    picked = dot(volume.T.astype(BF16), one_hot_t(vox, volume.shape[0]).astype(BF16))
    lane = iota((BLK, blocks), 1)
    weights = jnp.concatenate([jnp.where(lane < half, picked, 0.0), jnp.where(lane >= half, picked, 0.0)], 0)
    if sums:
        ones = jnp.concatenate([jnp.where(lane < half, 1.0, 0.0), jnp.where(lane >= half, 1.0, 0.0)], 0)
        weights = jnp.concatenate([weights, ones], 1)
    weights = weights.astype(BF16)
    width = weights.shape[1]
    column = lax.rem(iota((BLK, width), 1), half)

    def step(p, acc):
        pair = jnp.concatenate([proj[p], proj[p + half]], 1)
        return jnp.where(column == p, dot(pair, weights), acc)

    acc = jnp.zeros((BLK, width), F32)
    per = half // CHUNKS
    for c in range(CHUNKS):
        if before is not None:
            before(c)
        for p in range(c * per, (c + 1) * per):
            acc = step(p, acc)
    return acc


def products(proj, vectors, sums):
    blocks = proj.shape[0]
    group = 16
    row = iota((group, BLK), 0)
    tops, lows = [], []
    for g in range(blocks // group):
        mine = vectors[g * group:(g + 1) * group]
        left = jnp.concatenate([jnp.where(row == c, mine, 0.0) for c in range(group)], 1)
        if sums:
            ones = jnp.concatenate([jnp.where(row == c, 1.0, 0.0) for c in range(group)], 1)
            left = jnp.concatenate([left, ones], 0)
        right = proj[g * group:(g + 1) * group].reshape(group * BLK, BLK)
        out = dot(left.astype(BF16), right)
        tops.append(out[:group])
        if sums:
            lows.append(out[group:])
    columns = jnp.concatenate(tops, 0)
    return jnp.concatenate([columns, jnp.concatenate(lows, 0)], 1) if sums else columns


def collect(places, columns):
    return dot(jnp.concatenate([places] * 3, 1), jnp.concatenate(split3(columns), 0))


def backward(proj, weighted, rows, vox, vox_dev, sums):
    spots = one_hot_t(rows, weighted.shape[0])
    picked = dot(spots.T.astype(BF16), weighted.astype(BF16))
    stored = jnp.where(rows >= 0, 1.0, 0.0)
    places = (one_hot_t(vox, vox_dev) * stored).astype(BF16)
    return collect(places, products(proj, picked, sums))


def forward_turned(turned, volume, rows, vox, total):
    picked = dot(one_hot_t(vox, volume.shape[0]).T.astype(BF16), volume.astype(BF16))
    return collect(one_hot_t(rows, total).astype(BF16), products(turned, picked, False))


def turn_blocks(proj, turned):
    for k in range(proj.shape[0]):
        turned[k] = proj[k].T


def put_partial(sums, sino, mine, theirs, ray_dev):
    half = sums.shape[0] // 2
    slab = lax.axis_index("slab")
    core = lax.rem(slab, 2)
    top, low = sums[:half], sums[half:]
    mine[0:half, :] = -jnp.where(core == 0, top, low)
    theirs[0:half, :] = -jnp.where(core == 0, low, top)
    at = pl.ds(pl.multiple_of((slab >> 1) * ray_dev, 8), ray_dev)
    mine[at, :] = mine[at, :] + sino


def first_forward(slabs, capacity, ray_dev):
    def kernel(proj_hbm, vox_hbm, slot_hbm, ray_hbm, count_hbm, prior_hbm, sino_hbm,
               proj, vox, rows_out, prior, sino, mine, theirs, slot, ray, count, sems, small):
        blocks = proj_hbm.shape[0]
        half = blocks // 2
        per = half // CHUNKS
        smalls = [
            pltpu.make_async_copy(source, target, small.at[i])
            for i, (source, target) in enumerate([
                (vox_hbm, vox), (slot_hbm, slot), (ray_hbm, ray), (count_hbm, count),
                (prior_hbm, prior), (sino_hbm, sino),
            ])
        ]
        for copy in smalls:
            copy.start()
        copies = []
        for c in range(CHUNKS):
            for h in range(2):
                at = pl.ds(h * half + c * per, per)
                copy = pltpu.make_async_copy(proj_hbm.at[at], proj.at[at], sems.at[2 * c + h])
                copy.start()
                copies.append(copy)
        for copy in smalls:
            copy.wait()

        def before(c):
            copies[2 * c].wait()
            copies[2 * c + 1].wait()

        rows = block_rows(slot[...], ray[...], count[...], slabs, capacity, ray_dev)
        rows_out[...] = rows
        total = slabs * ray_dev
        columns = forward(proj, prior[...], vox[...], True, before)
        columns = jnp.concatenate([columns[:, :blocks].T, columns[:, blocks:].T], 1)
        both = collect(one_hot_t(rows, total).astype(BF16), columns)
        put_partial(both[:, :BLK], sino[...], mine, theirs, ray_dev)
        sums = both[:, BLK:]
        core = lax.rem(lax.axis_index("slab"), 2)
        top, low = sums[:total // 2], sums[total // 2:]
        mine[total // 2:total, :] = jnp.where(core == 0, top, low)
        theirs[total // 2:total, :] = jnp.where(core == 0, low, top)

    return kernel


def join_halves(mine, theirs):
    core = lax.rem(lax.axis_index("slab"), 2)
    mine, theirs = mine[...], theirs[...]
    return jnp.concatenate([jnp.where(core == 0, mine, theirs), jnp.where(core == 0, theirs, mine)], 0)


def first_backward(proj, rows, vox, mine, theirs, corr):
    vox_dev = corr.shape[0] // 2
    both = backward(proj, join_halves(mine, theirs), rows[...], vox[...], vox_dev, True)
    corr[0:vox_dev, :] = both[:, :BLK]
    corr[vox_dev:2 * vox_dev, :] = both[:, BLK:]


def next_forward(ray_dev):
    def kernel(proj, rows, vox, volume, corr, sino, volume_out, weight_out, mine, theirs):
        vox_dev = volume.shape[0]
        weights = 1.0 / jnp.maximum(corr[vox_dev:2 * vox_dev, :], 1.0)
        weight_out[...] = weights
        updated = volume[...] + weights * corr[0:vox_dev, :]
        volume_out[...] = updated
        sums = forward_turned(proj, updated, rows[...], vox[...], 2 * mine.shape[0])
        put_partial(sums, sino[...], mine, theirs, ray_dev)

    return kernel


def last_backward(proj, rows, vox, mine, theirs, corr):
    corr[...] = backward(proj, join_halves(mine, theirs), rows[...], vox[...], corr.shape[0], False)


def swap(x, axis, bit):
    size = lax.axis_size(axis)
    return lax.ppermute(x, axis, [(i, i ^ bit) for i in range(size)])


def over_slabs(mine, theirs):
    slabs = lax.axis_size("slab")
    x = mine + swap(theirs, "slab", 1)
    bits = [1 << b for b in range(1, slabs.bit_length() - 1)]
    while bits:
        if len(bits) == 1:
            x, bits = x + swap(x, "slab", bits[0]), []
            continue
        first, second, bits = bits[0], bits[1], bits[2:]
        x = (x + swap(x, "slab", first)) + (swap(x, "slab", second) + swap(x, "slab", first | second))
    return x


def over_angles(x, direct):
    angles = lax.axis_size("angle")
    bits = [1 << b for b in range(angles.bit_length() - 1)]
    while bits:
        if len(bits) == 1 or not direct:
            x, bits = x + swap(x, "angle", bits[0]), bits[1:]
            continue
        first, second, bits = bits[0], bits[1], bits[2:]
        x = (x + swap(x, "angle", first)) + (swap(x, "angle", second) + swap(x, "angle", first | second))
    return x


def local(projector, block_vox, block_slot, send_ray, block_count, prior, sinogram):
    slabs = lax.axis_size("slab")
    capacity = send_ray.shape[1] // slabs
    ray_dev = sinogram.shape[0]
    vox_dev = prior.shape[0]
    blocks = projector.shape[0]
    half = slabs * ray_dev // 2
    params = pltpu.CompilerParams(vmem_limit_bytes=8 * 1024 * 1024)
    vmem = lambda rows, dtype=F32: pltpu.VMEM((rows, BLK), dtype)
    line = pltpu.VMEM((1, blocks), jnp.int32)
    arguments = (
        projector, block_vox.reshape(1, blocks), block_slot.reshape(1, blocks), send_ray,
        block_count.reshape(1, 1), prior, sinogram,
    )

    proj, vox, rows, volume, sino, mine, theirs = pl.pallas_call(
        first_forward(slabs, capacity, ray_dev),
        out_shape=(
            pltpu.VMEM(projector.shape, BF16), line, line, vmem(vox_dev), vmem(ray_dev),
            vmem(2 * half), vmem(2 * half),
        ),
        in_specs=[whole(pl.ANY)] * 7,
        out_specs=(whole(),) * 7,
        scratch_shapes=[
            line,
            pltpu.VMEM(send_ray.shape, jnp.int32),
            pltpu.VMEM((1, 1), jnp.int32),
            pltpu.SemaphoreType.DMA((2 * CHUNKS,)),
            pltpu.SemaphoreType.DMA((6,)),
        ],
        compiler_params=params,
        name="first_forward",
    )(*[x if x.size == 1 else pltpu.with_memory_space_constraint(x, pltpu.HBM) for x in arguments])
    turned = pl.pallas_call(
        turn_blocks,
        out_shape=pltpu.VMEM(projector.shape, BF16),
        in_specs=[whole()],
        out_specs=whole(),
        compiler_params=params,
        cost_estimate=pl.CostEstimate(flops=0, bytes_accessed=2 * projector.size * 2, transcendentals=0),
        name="turn_blocks",
    )(proj)
    sums = over_slabs(mine, theirs)
    row_weight = 1.0 / jnp.maximum(sums[half:], 1.0)
    weighted = (row_weight * sums[:half]).astype(BF16)

    corr = pl.pallas_call(
        first_backward,
        out_shape=vmem(2 * vox_dev),
        in_specs=[whole()] * 5,
        out_specs=whole(),
        compiler_params=params,
        name="first_backward",
    )(proj, rows, vox, weighted, swap(weighted, "slab", 1))
    corr = over_angles(corr, False)

    volume, col_weight, mine, theirs = pl.pallas_call(
        next_forward(ray_dev),
        out_shape=(vmem(vox_dev), vmem(vox_dev), vmem(half), vmem(half)),
        in_specs=[whole()] * 6,
        out_specs=(whole(),) * 4,
        compiler_params=params,
        name="next_forward",
    )(turned, rows, vox, volume, corr, sino)
    residual = row_weight * over_slabs(mine, theirs)
    weighted = residual.astype(BF16)
    start = lax.div(lax.axis_index("slab"), 2) * ray_dev
    residual = lax.dynamic_slice_in_dim(residual, start, ray_dev)

    corr = pl.pallas_call(
        last_backward,
        out_shape=vmem(vox_dev),
        in_specs=[whole()] * 5,
        out_specs=whole(),
        compiler_params=params,
        name="last_backward",
    )(proj, rows, vox, weighted, swap(weighted, "slab", 1))
    corr = over_angles(corr, False)
    return volume + col_weight * corr, residual


def solution(mesh):
    return jax.shard_map(
        local,
        mesh=mesh,
        in_specs=(
            P(("slab", "angle"), None, None),
            P(("slab", "angle")),
            P(("slab", "angle")),
            P(("slab", "angle"), None),
            P(("slab", "angle")),
            P("slab", None),
            P(("slab", "angle"), None),
        ),
        out_specs=(P("slab", None), P(("slab", "angle"), None)),
        check_vma=False,
    )
```

```python
import jax
import jax.numpy as jnp
from jax import lax
from jax.experimental import pallas as pl
from jax.experimental.pallas import tpu as pltpu
from jax.sharding import PartitionSpec as P

ITERS = 2
F32 = jnp.float32
BF16 = jnp.bfloat16
BLK = 128
CHUNKS = 2


def whole(space=pltpu.VMEM):
    return pl.BlockSpec(memory_space=space)


def iota(shape, dim):
    return lax.broadcasted_iota(jnp.int32, shape, dim)


def split3(x):
    hi = x.astype(BF16)
    rest = x - hi.astype(F32)
    mid = rest.astype(BF16)
    low = (rest - mid.astype(F32)).astype(BF16)
    return hi, mid, low


def dot(a, b, dims=((1,), (0,))):
    return lax.dot_general(a, b, (dims, ((), ())), preferred_element_type=F32)


def one_hot_t(row, size):
    return jnp.where(iota((size, row.shape[1]), 0) == row, 1.0, 0.0)


def block_rows(slot, ray, count, slabs, capacity, ray_dev):
    slots = ray.shape[1]
    picks = one_hot_t(slot, slots).astype(BF16)
    rays = jnp.broadcast_to(ray, (16, slots)).astype(F32).astype(BF16)
    ray = dot(rays, picks)[0:1, :].astype(jnp.int32)
    owner = jnp.zeros_like(slot)
    for o in range(1, slabs):
        owner = owner + jnp.where(slot >= o * capacity, 1, 0)
    place = (owner & 1) * (slabs // 2) + (owner >> 1)
    stored = iota(slot.shape, 1) < count
    return jnp.where(stored, place * ray_dev + ray, -1)


def forward(proj, volume, vox, before):
    blocks = proj.shape[0]
    part = blocks // (2 * CHUNKS)
    picked = dot(volume.T.astype(BF16), one_hot_t(vox, volume.shape[0]).astype(BF16))
    first = lax.rem(iota((BLK, blocks), 1), 2 * part) < part
    halves = [jnp.where(side, jnp.concatenate([picked, jnp.ones_like(picked)], 1), 0.0)
              for side in (jnp.concatenate([first] * 2, 1), ~jnp.concatenate([first] * 2, 1))]
    weights = jnp.concatenate(halves, 0).astype(BF16)
    lane = lax.rem(iota((BLK, 2 * blocks), 1), blocks)
    column = lane - jnp.where(lax.rem(lane, 2 * part) < part, 0, part)
    acc = jnp.zeros((BLK, 2 * blocks), F32)
    for c in range(CHUNKS):
        before(c)
        for k in range(2 * part * c, 2 * part * c + part):
            pair = jnp.concatenate([proj[k], proj[k + part]], 1)
            acc = jnp.where(column == k, dot(pair, weights), acc)
    return acc


def products(proj, vectors, sums):
    blocks = proj.shape[0]
    group = 16
    row = iota((group, BLK), 0)
    tops, lows = [], []
    for g in range(blocks // group):
        mine = vectors[g * group:(g + 1) * group]
        left = jnp.concatenate([jnp.where(row == c, mine, 0.0) for c in range(group)], 1)
        if sums:
            ones = jnp.concatenate([jnp.where(row == c, 1.0, 0.0) for c in range(group)], 1)
            left = jnp.concatenate([left, ones], 0)
        right = proj[g * group:(g + 1) * group].reshape(group * BLK, BLK)
        out = dot(left.astype(BF16), right)
        tops.append(out[:group])
        if sums:
            lows.append(out[group:])
    columns = jnp.concatenate(tops, 0)
    return jnp.concatenate([columns, jnp.concatenate(lows, 0)], 1) if sums else columns


def collect(places, columns):
    return dot(jnp.concatenate([places] * 3, 1), jnp.concatenate(split3(columns), 0))


def backward(proj, weighted, picks, places, sums):
    return collect(places, products(proj, dot(picks, weighted), sums))


def forward_turned(turned, volume, picks, places):
    return collect(places, products(turned, dot(picks, volume.astype(BF16)), False))


def name_places(rows, vox, from_rays, to_rays, from_vox, to_vox):
    spots = one_hot_t(rows[...], to_rays.shape[0])
    from_rays[...] = spots.T.astype(BF16)
    to_rays[...] = spots.astype(BF16)
    spots = one_hot_t(vox[...], to_vox.shape[0])
    from_vox[...] = spots.T.astype(BF16)
    to_vox[...] = (spots * jnp.where(rows[...] >= 0, 1.0, 0.0)).astype(BF16)


def turn_blocks(proj, turned):
    for k in range(proj.shape[0]):
        turned[k] = proj[k].T


def put_partial(sums, sino, mine, theirs, ray_dev):
    half = sums.shape[0] // 2
    slab = lax.axis_index("slab")
    core = lax.rem(slab, 2)
    top, low = sums[:half], sums[half:]
    mine[0:half, :] = -jnp.where(core == 0, top, low)
    theirs[0:half, :] = -jnp.where(core == 0, low, top)
    at = pl.ds(pl.multiple_of((slab >> 1) * ray_dev, 8), ray_dev)
    mine[at, :] = mine[at, :] + sino


def first_forward(slabs, capacity, ray_dev):
    def kernel(proj_hbm, vox_hbm, slot_hbm, ray_hbm, count_hbm, prior_hbm, sino_hbm,
               proj, vox, rows_out, prior, sino, mine, theirs, slot, ray, count, sems, small):
        blocks = proj_hbm.shape[0]
        half = blocks // 2
        per = half // CHUNKS
        smalls = [
            pltpu.make_async_copy(source, target, small.at[i])
            for i, (source, target) in enumerate([
                (vox_hbm, vox), (slot_hbm, slot), (ray_hbm, ray), (count_hbm, count),
                (prior_hbm, prior), (sino_hbm, sino),
            ])
        ]
        copies = []
        size = blocks // CHUNKS
        for c in range(CHUNKS):
            at = pl.ds(c * size, size)
            copy = pltpu.make_async_copy(proj_hbm.at[at], proj.at[at], sems.at[c])
            copy.start()
            copies.append(copy)
            if not c:
                for copy in smalls:
                    copy.start()
        for copy in smalls:
            copy.wait()

        def before(c):
            copies[c].wait()

        rows = block_rows(slot[...], ray[...], count[...], slabs, capacity, ray_dev)
        rows_out[...] = rows
        total = slabs * ray_dev
        columns = forward(proj, prior[...], vox[...], before)
        columns = jnp.concatenate([columns[:, :blocks].T, columns[:, blocks:].T], 1)
        both = collect(one_hot_t(rows, total).astype(BF16), columns)
        put_partial(both[:, :BLK], sino[...], mine, theirs, ray_dev)
        sums = both[:, BLK:]
        core = lax.rem(lax.axis_index("slab"), 2)
        top, low = sums[:total // 2], sums[total // 2:]
        mine[total // 2:total, :] = jnp.where(core == 0, top, low)
        theirs[total // 2:total, :] = jnp.where(core == 0, low, top)

    return kernel


def join_halves(mine, theirs):
    core = lax.rem(lax.axis_index("slab"), 2)
    mine, theirs = mine[...], theirs[...]
    return jnp.concatenate([jnp.where(core == 0, mine, theirs), jnp.where(core == 0, theirs, mine)], 0)


def first_backward(proj, picks, places, mine, theirs, corr):
    vox_dev = corr.shape[0] // 2
    both = backward(proj, join_halves(mine, theirs), picks[...], places[...], True)
    corr[0:vox_dev, :] = both[:, :BLK]
    corr[vox_dev:2 * vox_dev, :] = both[:, BLK:]


def next_forward(ray_dev):
    def kernel(proj, picks, places, volume, corr, sino, volume_out, weight_out, mine, theirs):
        vox_dev = volume.shape[0]
        weights = 1.0 / jnp.maximum(corr[vox_dev:2 * vox_dev, :], 1.0)
        weight_out[...] = weights
        updated = volume[...] + weights * corr[0:vox_dev, :]
        volume_out[...] = updated
        sums = forward_turned(proj, updated, picks[...], places[...])
        put_partial(sums, sino[...], mine, theirs, ray_dev)

    return kernel


def last_backward(proj, picks, places, mine, theirs, corr):
    corr[...] = backward(proj, join_halves(mine, theirs), picks[...], places[...], False)


def swap(x, axis, bit):
    size = lax.axis_size(axis)
    return lax.ppermute(x, axis, [(i, i ^ bit) for i in range(size)])


def over_slabs(mine, theirs):
    slabs = lax.axis_size("slab")
    x = mine + swap(theirs, "slab", 1)
    bits = [1 << b for b in range(1, slabs.bit_length() - 1)]
    while bits:
        if len(bits) == 1:
            x, bits = x + swap(x, "slab", bits[0]), []
            continue
        first, second, bits = bits[0], bits[1], bits[2:]
        x = (x + swap(x, "slab", first)) + (swap(x, "slab", second) + swap(x, "slab", first | second))
    return x


def over_angles(x, direct):
    angles = lax.axis_size("angle")
    bits = [1 << b for b in range(angles.bit_length() - 1)]
    while bits:
        if len(bits) == 1 or not direct:
            x, bits = x + swap(x, "angle", bits[0]), bits[1:]
            continue
        first, second, bits = bits[0], bits[1], bits[2:]
        x = (x + swap(x, "angle", first)) + (swap(x, "angle", second) + swap(x, "angle", first | second))
    return x


def local(projector, block_vox, block_slot, send_ray, block_count, prior, sinogram):
    slabs = lax.axis_size("slab")
    capacity = send_ray.shape[1] // slabs
    ray_dev = sinogram.shape[0]
    vox_dev = prior.shape[0]
    blocks = projector.shape[0]
    half = slabs * ray_dev // 2
    params = pltpu.CompilerParams(vmem_limit_bytes=8 * 1024 * 1024)
    vmem = lambda rows, dtype=F32: pltpu.VMEM((rows, BLK), dtype)
    line = pltpu.VMEM((1, blocks), jnp.int32)
    arguments = (
        projector, block_vox.reshape(1, blocks), block_slot.reshape(1, blocks), send_ray,
        block_count.reshape(1, 1), prior, sinogram,
    )

    proj, vox, rows, volume, sino, mine, theirs = pl.pallas_call(
        first_forward(slabs, capacity, ray_dev),
        out_shape=(
            pltpu.VMEM(projector.shape, BF16), line, line, vmem(vox_dev), vmem(ray_dev),
            vmem(2 * half), vmem(2 * half),
        ),
        in_specs=[whole(pl.ANY)] * 7,
        out_specs=(whole(),) * 7,
        scratch_shapes=[
            line,
            pltpu.VMEM(send_ray.shape, jnp.int32),
            pltpu.VMEM((1, 1), jnp.int32),
            pltpu.SemaphoreType.DMA((2 * CHUNKS,)),
            pltpu.SemaphoreType.DMA((6,)),
        ],
        compiler_params=params,
        name="first_forward",
    )(*[x if x.size == 1 else pltpu.with_memory_space_constraint(x, pltpu.HBM) for x in arguments])
    from_rays, to_rays, from_vox, to_vox = pl.pallas_call(
        name_places,
        out_shape=(
            pltpu.VMEM((blocks, 2 * half), BF16), pltpu.VMEM((2 * half, blocks), BF16),
            pltpu.VMEM((blocks, vox_dev), BF16), pltpu.VMEM((vox_dev, blocks), BF16),
        ),
        in_specs=[whole()] * 2,
        out_specs=(whole(),) * 4,
        compiler_params=params,
        cost_estimate=pl.CostEstimate(flops=0, bytes_accessed=1 << 20, transcendentals=0),
        name="name_places",
    )(rows, vox)
    turned = pl.pallas_call(
        turn_blocks,
        out_shape=pltpu.VMEM(projector.shape, BF16),
        in_specs=[whole()],
        out_specs=whole(),
        compiler_params=params,
        cost_estimate=pl.CostEstimate(flops=0, bytes_accessed=2 * projector.size * 2, transcendentals=0),
        name="turn_blocks",
    )(proj)
    sums = over_slabs(mine, theirs)
    row_weight = 1.0 / jnp.maximum(sums[half:], 1.0)
    weighted = (row_weight * sums[:half]).astype(BF16)

    corr = pl.pallas_call(
        first_backward,
        out_shape=vmem(2 * vox_dev),
        in_specs=[whole()] * 5,
        out_specs=whole(),
        compiler_params=params,
        name="first_backward",
    )(proj, from_rays, to_vox, weighted, swap(weighted, "slab", 1))
    corr = over_angles(corr, False)

    volume, col_weight, mine, theirs = pl.pallas_call(
        next_forward(ray_dev),
        out_shape=(vmem(vox_dev), vmem(vox_dev), vmem(half), vmem(half)),
        in_specs=[whole()] * 6,
        out_specs=(whole(),) * 4,
        compiler_params=params,
        name="next_forward",
    )(turned, from_vox, to_rays, volume, corr, sino)
    residual = row_weight * over_slabs(mine, theirs)
    weighted = residual.astype(BF16)
    start = lax.div(lax.axis_index("slab"), 2) * ray_dev
    residual = lax.dynamic_slice_in_dim(residual, start, ray_dev)

    corr = pl.pallas_call(
        last_backward,
        out_shape=vmem(vox_dev),
        in_specs=[whole()] * 5,
        out_specs=whole(),
        compiler_params=params,
        name="last_backward",
    )(proj, from_rays, to_vox, weighted, swap(weighted, "slab", 1))
    corr = over_angles(corr, False)
    return volume + col_weight * corr, residual


def solution(mesh):
    return jax.shard_map(
        local,
        mesh=mesh,
        in_specs=(
            P(("slab", "angle"), None, None),
            P(("slab", "angle")),
            P(("slab", "angle")),
            P(("slab", "angle"), None),
            P(("slab", "angle")),
            P("slab", None),
            P(("slab", "angle"), None),
        ),
        out_specs=(P("slab", None), P(("slab", "angle"), None)),
        check_vma=False,
    )
```

```python
import jax
import jax.numpy as jnp
from jax import lax
from jax.experimental import pallas as pl
from jax.experimental.pallas import tpu as pltpu
from jax.sharding import PartitionSpec as P

ITERS = 2
F32 = jnp.float32
BF16 = jnp.bfloat16
BLK = 128
CHUNKS = 2


def whole(space=pltpu.VMEM):
    return pl.BlockSpec(memory_space=space)


def iota(shape, dim):
    return lax.broadcasted_iota(jnp.int32, shape, dim)


def split3(x):
    hi = x.astype(BF16)
    rest = x - hi.astype(F32)
    mid = rest.astype(BF16)
    low = (rest - mid.astype(F32)).astype(BF16)
    return hi, mid, low


def dot(a, b, dims=((1,), (0,))):
    return lax.dot_general(a, b, (dims, ((), ())), preferred_element_type=F32)


def one_hot_t(row, size):
    return jnp.where(iota((size, row.shape[1]), 0) == row, 1.0, 0.0)


def block_rows(slot, ray, count, slabs, capacity, ray_dev):
    slots = ray.shape[1]
    picks = one_hot_t(slot, slots).astype(BF16)
    rays = jnp.broadcast_to(ray, (16, slots)).astype(F32).astype(BF16)
    ray = dot(rays, picks)[0:1, :].astype(jnp.int32)
    owner = jnp.zeros_like(slot)
    for o in range(1, slabs):
        owner = owner + jnp.where(slot >= o * capacity, 1, 0)
    place = (owner & 1) * (slabs // 2) + (owner >> 1)
    stored = iota(slot.shape, 1) < count
    return jnp.where(stored, place * ray_dev + ray, -1)


def products(proj, vectors, sums=False, before=None, turn=False):
    blocks = proj.shape[0]
    group = 16
    row = iota((group, BLK), 0)
    tops, lows = [], []
    for g in range(blocks // group):
        if before is not None:
            before(g * group)
        mine = vectors[g * group:(g + 1) * group]
        left = jnp.concatenate([jnp.where(row == c, mine, 0.0) for c in range(group)], 1)
        if sums:
            ones = jnp.concatenate([jnp.where(row == c, 1.0, 0.0) for c in range(group)], 1)
            left = jnp.concatenate([left, ones], 0)
        if turn:
            right = jnp.concatenate([proj[k].T for k in range(g * group, (g + 1) * group)], 0)
        else:
            right = proj[g * group:(g + 1) * group].reshape(group * BLK, BLK)
        out = dot(left.astype(BF16), right)
        tops.append(out[:group])
        if sums:
            lows.append(out[group:])
    columns = jnp.concatenate(tops, 0)
    return jnp.concatenate([columns, jnp.concatenate(lows, 0)], 1) if sums else columns


def collect(places, columns):
    return dot(jnp.concatenate([places] * 3, 1), jnp.concatenate(split3(columns), 0))


def backward(proj, weighted, picks, places):
    return collect(places, products(proj, dot(picks, weighted)))


def forward_turned(turned, volume, picks, places):
    return collect(places, products(turned, dot(picks, volume.astype(BF16))))


def name_places(proj, rows, vox, from_rays, to_rays, from_vox, to_vox, columns):
    spots = one_hot_t(rows[...], to_rays.shape[0])
    from_rays[...] = spots.T.astype(BF16)
    to_rays[...] = spots.astype(BF16)
    spots = one_hot_t(vox[...], to_vox.shape[0])
    from_vox[...] = spots.T.astype(BF16)
    places = (spots * jnp.where(rows[...] >= 0, 1.0, 0.0)).astype(BF16)
    to_vox[...] = places
    columns[...] = collect(places, products(proj, jnp.ones((proj.shape[0], BLK), F32)))


def turn_blocks(proj, turned):
    for k in range(proj.shape[0]):
        turned[k] = proj[k].T


def put_partial(sums, sino, mine, theirs, ray_dev):
    half = sums.shape[0] // 2
    slab = lax.axis_index("slab")
    core = lax.rem(slab, 2)
    top, low = sums[:half], sums[half:]
    mine[0:half, :] = -jnp.where(core == 0, top, low)
    theirs[0:half, :] = -jnp.where(core == 0, low, top)
    at = pl.ds(pl.multiple_of((slab >> 1) * ray_dev, 8), ray_dev)
    mine[at, :] = mine[at, :] + sino


def first_forward(slabs, capacity, ray_dev):
    def kernel(proj_hbm, vox_hbm, slot_hbm, ray_hbm, count_hbm, prior_hbm, sino_hbm,
               proj, vox, rows_out, prior, sino, mine, theirs, slot, ray, count, sems, small):
        blocks = proj_hbm.shape[0]
        half = blocks // 2
        per = half // CHUNKS
        smalls = [
            pltpu.make_async_copy(source, target, small.at[i])
            for i, (source, target) in enumerate([
                (vox_hbm, vox), (slot_hbm, slot), (ray_hbm, ray), (count_hbm, count),
                (prior_hbm, prior), (sino_hbm, sino),
            ])
        ]
        copies = []
        size = blocks // CHUNKS
        for c in range(CHUNKS):
            at = pl.ds(c * size, size)
            copy = pltpu.make_async_copy(proj_hbm.at[at], proj.at[at], sems.at[c])
            copy.start()
            copies.append(copy)
            if not c:
                for copy in smalls:
                    copy.start()
        for copy in smalls:
            copy.wait()

        def before(k):
            if k % size == 0:
                copies[k // size].wait()

        rows = block_rows(slot[...], ray[...], count[...], slabs, capacity, ray_dev)
        rows_out[...] = rows
        total = slabs * ray_dev
        picks = one_hot_t(vox[...], prior.shape[0]).T.astype(BF16)
        columns = products(proj, dot(picks, prior[...].astype(BF16)), True, before, True)
        both = collect(one_hot_t(rows, total).astype(BF16), columns)
        put_partial(both[:, :BLK], sino[...], mine, theirs, ray_dev)
        sums = both[:, BLK:]
        core = lax.rem(lax.axis_index("slab"), 2)
        top, low = sums[:total // 2], sums[total // 2:]
        mine[total // 2:total, :] = jnp.where(core == 0, top, low)
        theirs[total // 2:total, :] = jnp.where(core == 0, low, top)

    return kernel


def join_halves(mine, theirs):
    core = lax.rem(lax.axis_index("slab"), 2)
    mine, theirs = mine[...], theirs[...]
    return jnp.concatenate([jnp.where(core == 0, mine, theirs), jnp.where(core == 0, theirs, mine)], 0)


def next_forward(ray_dev):
    def kernel(proj, picks, places, volume, corr, col_total, sino, volume_out, weight_out, mine, theirs):
        weights = 1.0 / jnp.maximum(col_total[...], 1.0)
        weight_out[...] = weights
        updated = volume[...] + weights * corr[...]
        volume_out[...] = updated
        sums = forward_turned(proj, updated, picks[...], places[...])
        put_partial(sums, sino[...], mine, theirs, ray_dev)

    return kernel


def to_voxels(proj, picks, places, mine, theirs, corr):
    corr[...] = backward(proj, join_halves(mine, theirs), picks[...], places[...])


def swap(x, axis, bit):
    size = lax.axis_size(axis)
    return lax.ppermute(x, axis, [(i, i ^ bit) for i in range(size)])


def over_slabs(mine, theirs, beside=None):
    slabs = lax.axis_size("slab")
    x = mine + swap(theirs, "slab", 1)
    bits = [1 << b for b in range(1, slabs.bit_length() - 1)]
    while bits:
        if len(bits) == 1:
            x, bits = x + swap(x, "slab", bits[0]), []
            continue
        first, second, bits = bits[0], bits[1], bits[2:]
        near = swap(x, "slab", first)
        other = swap(x, "slab", second) , swap(x, "slab", first | second)
        if beside is not None and not bits:
            near, beside = lax.optimization_barrier((near, beside))
            beside = beside + swap(beside, "angle", 1)
        x = (x + near) + (other[0] + other[1])
    return x if beside is None else (x, beside)


def over_angles(x, done=0):
    angles = lax.axis_size("angle")
    for b in range(done, angles.bit_length() - 1):
        x = x + swap(x, "angle", 1 << b)
    return x


def local(projector, block_vox, block_slot, send_ray, block_count, prior, sinogram):
    slabs = lax.axis_size("slab")
    capacity = send_ray.shape[1] // slabs
    ray_dev = sinogram.shape[0]
    vox_dev = prior.shape[0]
    blocks = projector.shape[0]
    half = slabs * ray_dev // 2
    params = pltpu.CompilerParams(vmem_limit_bytes=8 * 1024 * 1024)
    vmem = lambda rows, dtype=F32: pltpu.VMEM((rows, BLK), dtype)
    line = pltpu.VMEM((1, blocks), jnp.int32)
    arguments = (
        projector, block_vox.reshape(1, blocks), block_slot.reshape(1, blocks), send_ray,
        block_count.reshape(1, 1), prior, sinogram,
    )

    proj, vox, rows, volume, sino, mine, theirs = pl.pallas_call(
        first_forward(slabs, capacity, ray_dev),
        out_shape=(
            pltpu.VMEM(projector.shape, BF16), line, line, vmem(vox_dev), vmem(ray_dev),
            vmem(2 * half), vmem(2 * half),
        ),
        in_specs=[whole(pl.ANY)] * 7,
        out_specs=(whole(),) * 7,
        scratch_shapes=[
            line,
            pltpu.VMEM(send_ray.shape, jnp.int32),
            pltpu.VMEM((1, 1), jnp.int32),
            pltpu.SemaphoreType.DMA((2 * CHUNKS,)),
            pltpu.SemaphoreType.DMA((6,)),
        ],
        compiler_params=params,
        name="first_forward",
    )(*[x if x.size == 1 else pltpu.with_memory_space_constraint(x, pltpu.HBM) for x in arguments])
    from_rays, to_rays, from_vox, to_vox, col_total = pl.pallas_call(
        name_places,
        out_shape=(
            pltpu.VMEM((blocks, 2 * half), BF16), pltpu.VMEM((2 * half, blocks), BF16),
            pltpu.VMEM((blocks, vox_dev), BF16), pltpu.VMEM((vox_dev, blocks), BF16), vmem(vox_dev),
        ),
        in_specs=[whole()] * 3,
        out_specs=(whole(),) * 5,
        compiler_params=params,
        cost_estimate=pl.CostEstimate(flops=0, bytes_accessed=1 << 20, transcendentals=0),
        name="name_places",
    )(proj, rows, vox)
    turned = pl.pallas_call(
        turn_blocks,
        out_shape=pltpu.VMEM(projector.shape, BF16),
        in_specs=[whole()],
        out_specs=whole(),
        compiler_params=params,
        cost_estimate=pl.CostEstimate(flops=0, bytes_accessed=2 * projector.size * 2, transcendentals=0),
        name="turn_blocks",
    )(proj)
    sums, col_total = over_slabs(mine, theirs, col_total)
    col_total = over_angles(col_total, 1)
    row_weight = 1.0 / jnp.maximum(sums[half:], 1.0)
    weighted = (row_weight * sums[:half]).astype(BF16)

    corr = pl.pallas_call(
        to_voxels,
        out_shape=vmem(vox_dev),
        in_specs=[whole()] * 5,
        out_specs=whole(),
        compiler_params=params,
        name="first_backward",
    )(proj, from_rays, to_vox, weighted, swap(weighted, "slab", 1))
    corr = over_angles(corr)

    volume, col_weight, mine, theirs = pl.pallas_call(
        next_forward(ray_dev),
        out_shape=(vmem(vox_dev), vmem(vox_dev), vmem(half), vmem(half)),
        in_specs=[whole()] * 7,
        out_specs=(whole(),) * 4,
        compiler_params=params,
        name="next_forward",
    )(turned, from_vox, to_rays, volume, corr, col_total, sino)
    residual = row_weight * over_slabs(mine, theirs)
    weighted = residual.astype(BF16)
    start = lax.div(lax.axis_index("slab"), 2) * ray_dev
    residual = lax.dynamic_slice_in_dim(residual, start, ray_dev)

    corr = pl.pallas_call(
        to_voxels,
        out_shape=vmem(vox_dev),
        in_specs=[whole()] * 5,
        out_specs=whole(),
        compiler_params=params,
        name="last_backward",
    )(proj, from_rays, to_vox, weighted, swap(weighted, "slab", 1))
    corr = over_angles(corr)
    return volume + col_weight * corr, residual


def solution(mesh):
    return jax.shard_map(
        local,
        mesh=mesh,
        in_specs=(
            P(("slab", "angle"), None, None),
            P(("slab", "angle")),
            P(("slab", "angle")),
            P(("slab", "angle"), None),
            P(("slab", "angle")),
            P("slab", None),
            P(("slab", "angle"), None),
        ),
        out_specs=(P("slab", None), P(("slab", "angle"), None)),
        check_vma=False,
    )
```

```python
import jax
import jax.numpy as jnp
from jax import lax
from jax.experimental import pallas as pl
from jax.experimental.pallas import tpu as pltpu
from jax.sharding import PartitionSpec as P

ITERS = 2
F32 = jnp.float32
BF16 = jnp.bfloat16
BLK = 128
CHUNKS = 2


def whole(space=pltpu.VMEM):
    return pl.BlockSpec(memory_space=space)


def iota(shape, dim):
    return lax.broadcasted_iota(jnp.int32, shape, dim)


def split3(x):
    hi = x.astype(BF16)
    rest = x - hi.astype(F32)
    mid = rest.astype(BF16)
    low = (rest - mid.astype(F32)).astype(BF16)
    return hi, mid, low


def dot(a, b, dims=((1,), (0,))):
    return lax.dot_general(a, b, (dims, ((), ())), preferred_element_type=F32)


def one_hot_t(row, size):
    return jnp.where(iota((size, row.shape[1]), 0) == row, 1.0, 0.0)


def block_rows(slot, ray, count, slabs, capacity, ray_dev):
    slots = ray.shape[1]
    picks = one_hot_t(slot, slots).astype(BF16)
    rays = jnp.broadcast_to(ray, (16, slots)).astype(F32).astype(BF16)
    ray = dot(rays, picks)[0:1, :].astype(jnp.int32)
    owner = jnp.zeros_like(slot)
    for o in range(1, slabs):
        owner = owner + jnp.where(slot >= o * capacity, 1, 0)
    place = (owner & 1) * (slabs // 2) + (owner >> 1)
    stored = iota(slot.shape, 1) < count
    return jnp.where(stored, place * ray_dev + ray, -1)


def products(proj, vectors, sums=False, before=None, turn=False):
    blocks = proj.shape[0]
    group = 16
    row = iota((group, BLK), 0)
    tops, lows = [], []
    for g in range(blocks // group):
        if before is not None:
            before(g * group)
        mine = vectors[g * group:(g + 1) * group]
        left = jnp.concatenate([jnp.where(row == c, mine, 0.0) for c in range(group)], 1)
        if sums:
            ones = jnp.concatenate([jnp.where(row == c, 1.0, 0.0) for c in range(group)], 1)
            left = jnp.concatenate([left, ones], 0)
        if turn:
            right = jnp.concatenate([proj[k].T for k in range(g * group, (g + 1) * group)], 0)
        else:
            right = proj[g * group:(g + 1) * group].reshape(group * BLK, BLK)
        out = dot(left.astype(BF16), right)
        tops.append(out[:group])
        if sums:
            lows.append(out[group:])
    columns = jnp.concatenate(tops, 0)
    return jnp.concatenate([columns, jnp.concatenate(lows, 0)], 1) if sums else columns


def collect(places, columns):
    return dot(jnp.concatenate([places] * 3, 1), jnp.concatenate(split3(columns), 0))


def backward(proj, weighted, picks, places):
    return collect(places, products(proj, dot(picks, weighted)))


def forward_turned(turned, volume, picks, places):
    return collect(places, products(turned, dot(picks, volume.astype(BF16))))


def name_places(proj, rows, vox, from_rays, to_rays, from_vox, to_vox, columns):
    spots = one_hot_t(rows[...], to_rays.shape[0])
    from_rays[...] = spots.T.astype(BF16)
    to_rays[...] = spots.astype(BF16)
    spots = one_hot_t(vox[...], to_vox.shape[0])
    from_vox[...] = spots.T.astype(BF16)
    places = (spots * jnp.where(rows[...] >= 0, 1.0, 0.0)).astype(BF16)
    to_vox[...] = places
    columns[...] = collect(places, products(proj, jnp.ones((proj.shape[0], BLK), F32)))


def turn_blocks(proj, turned):
    for k in range(proj.shape[0]):
        turned[k] = proj[k].T


def last_to_voxels(early, late, picks, places, mine, theirs, corr):
    picked = dot(picks[...], join_halves(mine, theirs))
    count = early.shape[0]
    columns = [products(early, picked[:count]), products(late, picked[count:])]
    corr[...] = collect(places[...], jnp.concatenate(columns, 0))


def last_update(volume, weight, corr, far, mid, near, out):
    out[...] = volume[...] + weight[...] * ((corr[...] + near[...]) + (mid[...] + far[...]))


def fetch_blocks(start):
    def kernel(proj_hbm, proj, sem):
        copy = pltpu.make_async_copy(proj_hbm.at[pl.ds(start, proj.shape[0])], proj, sem)
        copy.start()
        copy.wait()

    return kernel


def put_partial(sums, sino, mine, theirs, ray_dev):
    half = sums.shape[0] // 2
    slab = lax.axis_index("slab")
    core = lax.rem(slab, 2)
    top, low = sums[:half], sums[half:]
    mine[0:half, :] = -jnp.where(core == 0, top, low)
    theirs[0:half, :] = -jnp.where(core == 0, low, top)
    at = pl.ds(pl.multiple_of((slab >> 1) * ray_dev, 8), ray_dev)
    mine[at, :] = mine[at, :] + sino


def first_forward(slabs, capacity, ray_dev):
    def kernel(proj_hbm, vox_hbm, slot_hbm, ray_hbm, count_hbm, prior_hbm, sino_hbm,
               proj, vox, rows_out, prior, sino, mine, theirs, slot, ray, count, sems, small):
        blocks = proj_hbm.shape[0]
        half = blocks // 2
        per = half // CHUNKS
        smalls = [
            pltpu.make_async_copy(source, target, small.at[i])
            for i, (source, target) in enumerate([
                (vox_hbm, vox), (slot_hbm, slot), (ray_hbm, ray), (count_hbm, count),
                (prior_hbm, prior), (sino_hbm, sino),
            ])
        ]
        copies = []
        size = blocks // CHUNKS
        for c in range(CHUNKS):
            at = pl.ds(c * size, size)
            copy = pltpu.make_async_copy(proj_hbm.at[at], proj.at[at], sems.at[c])
            copy.start()
            copies.append(copy)
            if not c:
                for copy in smalls:
                    copy.start()
        for copy in smalls:
            copy.wait()

        def before(k):
            if k % size == 0:
                copies[k // size].wait()

        rows = block_rows(slot[...], ray[...], count[...], slabs, capacity, ray_dev)
        rows_out[...] = rows
        total = slabs * ray_dev
        picks = one_hot_t(vox[...], prior.shape[0]).T.astype(BF16)
        columns = products(proj, dot(picks, prior[...].astype(BF16)), True, before, True)
        both = collect(one_hot_t(rows, total).astype(BF16), columns)
        put_partial(both[:, :BLK], sino[...], mine, theirs, ray_dev)
        sums = both[:, BLK:]
        core = lax.rem(lax.axis_index("slab"), 2)
        top, low = sums[:total // 2], sums[total // 2:]
        mine[total // 2:total, :] = jnp.where(core == 0, top, low)
        theirs[total // 2:total, :] = jnp.where(core == 0, low, top)

    return kernel


def join_halves(mine, theirs):
    core = lax.rem(lax.axis_index("slab"), 2)
    mine, theirs = mine[...], theirs[...]
    return jnp.concatenate([jnp.where(core == 0, mine, theirs), jnp.where(core == 0, theirs, mine)], 0)


def next_forward(ray_dev):
    def kernel(proj, picks, places, volume, corr, col_total, sino, volume_out, weight_out, mine, theirs):
        weights = 1.0 / jnp.maximum(col_total[...], 1.0)
        weight_out[...] = weights
        updated = volume[...] + weights * corr[...]
        volume_out[...] = updated
        sums = forward_turned(proj, updated, picks[...], places[...])
        put_partial(sums, sino[...], mine, theirs, ray_dev)

    return kernel


def to_voxels(proj, picks, places, mine, theirs, corr):
    corr[...] = backward(proj, join_halves(mine, theirs), picks[...], places[...])


def swap(x, axis, bit):
    size = lax.axis_size(axis)
    return lax.ppermute(x, axis, [(i, i ^ bit) for i in range(size)])


def over_slabs(mine, theirs, beside=None, after=None):
    slabs = lax.axis_size("slab")
    x = mine + swap(theirs, "slab", 1)
    if after is not None:
        x, after = lax.optimization_barrier((x, after))
    bits = [1 << b for b in range(1, slabs.bit_length() - 1)]
    waiting = beside is not None
    while bits:
        if len(bits) == 1:
            x, bits = x + swap(x, "slab", bits[0]), []
            continue
        first, second, bits = bits[0], bits[1], bits[2:]
        near = swap(x, "slab", first)
        other = swap(x, "slab", second), swap(x, "slab", first | second)
        if waiting and not bits:
            near, beside = lax.optimization_barrier((near, beside))
            beside, waiting = beside + swap(beside, "angle", 1), False
        x = (x + near) + (other[0] + other[1])
    if waiting:
        beside = beside + swap(beside, "angle", 1)
    return x, after if beside is None else beside


def over_angles(x, done=0):
    angles = lax.axis_size("angle")
    for b in range(done, angles.bit_length() - 1):
        x = x + swap(x, "angle", 1 << b)
    return x


def local(projector, block_vox, block_slot, send_ray, block_count, prior, sinogram):
    slabs = lax.axis_size("slab")
    capacity = send_ray.shape[1] // slabs
    ray_dev = sinogram.shape[0]
    vox_dev = prior.shape[0]
    blocks = projector.shape[0]
    half = slabs * ray_dev // 2
    params = pltpu.CompilerParams(vmem_limit_bytes=8 * 1024 * 1024)
    vmem = lambda rows, dtype=F32: pltpu.VMEM((rows, BLK), dtype)
    line = pltpu.VMEM((1, blocks), jnp.int32)
    arguments = (
        projector, block_vox.reshape(1, blocks), block_slot.reshape(1, blocks), send_ray,
        block_count.reshape(1, 1), prior, sinogram,
    )

    proj, vox, rows, volume, sino, mine, theirs = pl.pallas_call(
        first_forward(slabs, capacity, ray_dev),
        out_shape=(
            pltpu.VMEM(projector.shape, BF16), line, line, vmem(vox_dev), vmem(ray_dev),
            vmem(2 * half), vmem(2 * half),
        ),
        in_specs=[whole(pl.ANY)] * 7,
        out_specs=(whole(),) * 7,
        scratch_shapes=[
            line,
            pltpu.VMEM(send_ray.shape, jnp.int32),
            pltpu.VMEM((1, 1), jnp.int32),
            pltpu.SemaphoreType.DMA((2 * CHUNKS,)),
            pltpu.SemaphoreType.DMA((6,)),
        ],
        compiler_params=params,
        name="first_forward",
    )(*[x if x.size == 1 else pltpu.with_memory_space_constraint(x, pltpu.HBM) for x in arguments])
    from_rays, to_rays, from_vox, to_vox, col_total = pl.pallas_call(
        name_places,
        out_shape=(
            pltpu.VMEM((blocks, 2 * half), BF16), pltpu.VMEM((2 * half, blocks), BF16),
            pltpu.VMEM((blocks, vox_dev), BF16), pltpu.VMEM((vox_dev, blocks), BF16), vmem(vox_dev),
        ),
        in_specs=[whole()] * 3,
        out_specs=(whole(),) * 5,
        compiler_params=params,
        cost_estimate=pl.CostEstimate(flops=0, bytes_accessed=1 << 20, transcendentals=0),
        name="name_places",
    )(proj, rows, vox)
    turned = pl.pallas_call(
        turn_blocks,
        out_shape=pltpu.VMEM(projector.shape, BF16),
        in_specs=[whole()],
        out_specs=whole(),
        compiler_params=params,
        cost_estimate=pl.CostEstimate(flops=0, bytes_accessed=2 * projector.size * 2, transcendentals=0),
        name="turn_blocks",
    )(proj)
    sums, col_total = over_slabs(mine, theirs, col_total)
    col_total = over_angles(col_total, 1)
    row_weight = 1.0 / jnp.maximum(sums[half:], 1.0)
    weighted = (row_weight * sums[:half]).astype(BF16)

    corr = pl.pallas_call(
        to_voxels,
        out_shape=vmem(vox_dev),
        in_specs=[whole()] * 5,
        out_specs=whole(),
        compiler_params=params,
        name="first_backward",
    )(proj, from_rays, to_vox, weighted, swap(weighted, "slab", 1))
    corr = over_angles(corr)

    volume, col_weight, mine, theirs = pl.pallas_call(
        next_forward(ray_dev),
        out_shape=(vmem(vox_dev), vmem(vox_dev), vmem(half), vmem(half)),
        in_specs=[whole()] * 7,
        out_specs=(whole(),) * 4,
        compiler_params=params,
        name="next_forward",
    )(turned, from_vox, to_rays, volume, corr, col_total, sino)
    residual, projector = over_slabs(mine, theirs, None, projector)
    count = blocks * 3 // 4
    fetched = [
        pl.pallas_call(
            fetch_blocks(low),
            out_shape=pltpu.VMEM((size,) + projector.shape[1:], BF16),
            in_specs=[whole(pl.ANY)],
            out_specs=whole(),
            scratch_shapes=[pltpu.SemaphoreType.DMA],
            compiler_params=params,
            cost_estimate=pl.CostEstimate(flops=0, bytes_accessed=size << 16, transcendentals=0),
            name="fetch_blocks",
        )(pltpu.with_memory_space_constraint(projector, pltpu.HBM))
        for low, size in ((0, count), (count, blocks - count))
    ]
    early, late = fetched
    residual, early = lax.optimization_barrier((residual, early))
    residual = row_weight * residual
    weighted = residual.astype(BF16)
    start = lax.div(lax.axis_index("slab"), 2) * ray_dev
    residual = lax.dynamic_slice_in_dim(residual, start, ray_dev)

    corr = pl.pallas_call(
        last_to_voxels,
        out_shape=vmem(vox_dev),
        in_specs=[whole()] * 6,
        out_specs=whole(),
        compiler_params=params,
        name="last_backward",
    )(early, late, from_rays, to_vox, weighted, swap(weighted, "slab", 1))
    corr = over_angles(corr, 2)
    far, mid, near = (swap(corr, "angle", bit) for bit in (3, 2, 1))
    volume = pl.pallas_call(
        last_update,
        out_shape=jax.ShapeDtypeStruct((vox_dev, BLK), F32),
        in_specs=[whole()] * 6,
        out_specs=whole(),
        compiler_params=params,
        name="last_update",
    )(volume, col_weight, corr, far, mid, near)
    return volume, residual


def solution(mesh):
    return jax.shard_map(
        local,
        mesh=mesh,
        in_specs=(
            P(("slab", "angle"), None, None),
            P(("slab", "angle")),
            P(("slab", "angle")),
            P(("slab", "angle"), None),
            P(("slab", "angle")),
            P("slab", None),
            P(("slab", "angle"), None),
        ),
        out_specs=(P("slab", None), P(("slab", "angle"), None)),
        check_vma=False,
    )
```

```python
import jax
import jax.numpy as jnp
from jax import lax
from jax.experimental import pallas as pl
from jax.experimental.pallas import tpu as pltpu
from jax.sharding import PartitionSpec as P

ITERS = 2
F32 = jnp.float32
BF16 = jnp.bfloat16
BLK = 128
CHUNKS = 2
ORDER = (1, 2, 3)


def whole(space=pltpu.VMEM):
    return pl.BlockSpec(memory_space=space)


def iota(shape, dim):
    return lax.broadcasted_iota(jnp.int32, shape, dim)


def split3(x):
    hi = x.astype(BF16)
    rest = x - hi.astype(F32)
    mid = rest.astype(BF16)
    low = (rest - mid.astype(F32)).astype(BF16)
    return hi, mid, low


def dot(a, b, dims=((1,), (0,))):
    return lax.dot_general(a, b, (dims, ((), ())), preferred_element_type=F32)


def one_hot_t(row, size):
    return jnp.where(iota((size, row.shape[1]), 0) == row, 1.0, 0.0)


def block_rows(slot, ray, count, slabs, capacity, ray_dev):
    slots = ray.shape[1]
    picks = one_hot_t(slot, slots).astype(BF16)
    rays = jnp.broadcast_to(ray, (16, slots)).astype(F32).astype(BF16)
    ray = dot(rays, picks)[0:1, :].astype(jnp.int32)
    owner = jnp.zeros_like(slot)
    for o in range(1, slabs):
        owner = owner + jnp.where(slot >= o * capacity, 1, 0)
    place = (owner & 1) * (slabs // 2) + (owner >> 1)
    stored = iota(slot.shape, 1) < count
    return jnp.where(stored, place * ray_dev + ray, -1)


def products(proj, vectors, sums=False, before=None, turn=False):
    blocks = proj.shape[0]
    group = 16
    row = iota((group, BLK), 0)
    tops, lows = [], []
    for g in range(blocks // group):
        if before is not None:
            before(g * group)
        mine = vectors[g * group:(g + 1) * group]
        left = jnp.concatenate([jnp.where(row == c, mine, 0.0) for c in range(group)], 1)
        if sums:
            ones = jnp.concatenate([jnp.where(row == c, 1.0, 0.0) for c in range(group)], 1)
            left = jnp.concatenate([left, ones], 0)
        if turn:
            right = jnp.concatenate([proj[k].T for k in range(g * group, (g + 1) * group)], 0)
        else:
            right = proj[g * group:(g + 1) * group].reshape(group * BLK, BLK)
        out = dot(left.astype(BF16), right)
        tops.append(out[:group])
        if sums:
            lows.append(out[group:])
    columns = jnp.concatenate(tops, 0)
    return jnp.concatenate([columns, jnp.concatenate(lows, 0)], 1) if sums else columns


def collect(places, columns):
    return dot(jnp.concatenate([places] * 3, 1), jnp.concatenate(split3(columns), 0))


def backward(proj, weighted, picks, places):
    return collect(places, products(proj, dot(picks, weighted)))


def forward_turned(turned, volume, picks, places):
    return collect(places, products(turned, dot(picks, volume.astype(BF16))))


def name_places(proj, rows, vox, from_rays, to_rays, from_vox, to_vox, columns):
    spots = one_hot_t(rows[...], to_rays.shape[0])
    from_rays[...] = spots.T.astype(BF16)
    to_rays[...] = spots.astype(BF16)
    spots = one_hot_t(vox[...], to_vox.shape[0])
    from_vox[...] = spots.T.astype(BF16)
    places = (spots * jnp.where(rows[...] >= 0, 1.0, 0.0)).astype(BF16)
    to_vox[...] = places
    columns[...] = collect(places, products(proj, jnp.ones((proj.shape[0], BLK), F32)))


def turn_blocks(proj, turned):
    for k in range(proj.shape[0]):
        turned[k] = proj[k].T


def last_to_voxels(early, late, picks, places, mine, theirs, corr):
    picked = dot(picks[...], join_halves(mine, theirs))
    count = early.shape[0]
    columns = [products(early, picked[:count]), products(late, picked[count:])]
    corr[...] = collect(places[...], jnp.concatenate(columns, 0))


def last_update(volume, weight, corr, near, mid, far, out):
    out[...] = volume[...] + weight[...] * ((corr[...] + near[...]) + (mid[...] + far[...]))


def fetch_blocks(start):
    def kernel(proj_hbm, proj, sem):
        copy = pltpu.make_async_copy(proj_hbm.at[pl.ds(start, proj.shape[0])], proj, sem)
        copy.start()
        copy.wait()

    return kernel


def put_partial(sums, sino, mine, theirs, ray_dev):
    half = sums.shape[0] // 2
    slab = lax.axis_index("slab")
    core = lax.rem(slab, 2)
    top, low = sums[:half], sums[half:]
    mine[0:half, :] = -jnp.where(core == 0, top, low)
    theirs[0:half, :] = -jnp.where(core == 0, low, top)
    at = pl.ds(pl.multiple_of((slab >> 1) * ray_dev, 8), ray_dev)
    mine[at, :] = mine[at, :] + sino


def first_forward(slabs, capacity, ray_dev):
    def kernel(proj_hbm, vox_hbm, slot_hbm, ray_hbm, count_hbm, prior_hbm, sino_hbm,
               proj, vox, rows_out, prior, sino, mine, theirs, slot, ray, count, sems, small):
        blocks = proj_hbm.shape[0]
        half = blocks // 2
        per = half // CHUNKS
        smalls = [
            pltpu.make_async_copy(source, target, small.at[i])
            for i, (source, target) in enumerate([
                (vox_hbm, vox), (slot_hbm, slot), (ray_hbm, ray), (count_hbm, count),
                (prior_hbm, prior), (sino_hbm, sino),
            ])
        ]
        copies = []
        size = blocks // CHUNKS
        for c in range(CHUNKS):
            at = pl.ds(c * size, size)
            copy = pltpu.make_async_copy(proj_hbm.at[at], proj.at[at], sems.at[c])
            copy.start()
            copies.append(copy)
            if not c:
                for copy in smalls:
                    copy.start()
        for copy in smalls:
            copy.wait()

        def before(k):
            if k % size == 0:
                copies[k // size].wait()

        rows = block_rows(slot[...], ray[...], count[...], slabs, capacity, ray_dev)
        rows_out[...] = rows
        total = slabs * ray_dev
        picks = one_hot_t(vox[...], prior.shape[0]).T.astype(BF16)
        columns = products(proj, dot(picks, prior[...].astype(BF16)), True, before, True)
        both = collect(one_hot_t(rows, total).astype(BF16), columns)
        put_partial(both[:, :BLK], sino[...], mine, theirs, ray_dev)
        sums = both[:, BLK:]
        core = lax.rem(lax.axis_index("slab"), 2)
        top, low = sums[:total // 2], sums[total // 2:]
        mine[total // 2:total, :] = jnp.where(core == 0, top, low)
        theirs[total // 2:total, :] = jnp.where(core == 0, low, top)

    return kernel


def join_halves(mine, theirs):
    core = lax.rem(lax.axis_index("slab"), 2)
    mine, theirs = mine[...], theirs[...]
    return jnp.concatenate([jnp.where(core == 0, mine, theirs), jnp.where(core == 0, theirs, mine)], 0)


def next_forward(ray_dev):
    def kernel(proj, picks, places, volume, own, near, mid, far, sino, volume_out, weight_out, mine, theirs):
        vox_dev = volume.shape[0]
        sums = (own[...] + near[...]) + (mid[...] + far[...])
        weights = 1.0 / jnp.maximum(sums[vox_dev:], 1.0)
        weight_out[...] = weights
        updated = volume[...] + weights * sums[:vox_dev]
        volume_out[...] = updated
        sums = forward_turned(proj, updated, picks[...], places[...])
        put_partial(sums, sino[...], mine, theirs, ray_dev)

    return kernel


def first_backward(proj, picks, places, mine, theirs, col_total, corr):
    vox_dev = col_total.shape[0]
    corr[0:vox_dev, :] = backward(proj, join_halves(mine, theirs), picks[...], places[...])
    corr[vox_dev:2 * vox_dev, :] = col_total[...]


def swap(x, axis, bit):
    size = lax.axis_size(axis)
    return lax.ppermute(x, axis, [(i, i ^ bit) for i in range(size)])


def over_slabs(mine, theirs, after=None):
    slabs = lax.axis_size("slab")
    x = mine + swap(theirs, "slab", 1)
    if after is not None:
        x, after = lax.optimization_barrier((x, after))
    bits = [1 << b for b in range(1, slabs.bit_length() - 1)]
    while bits:
        if len(bits) == 1:
            x, bits = x + swap(x, "slab", bits[0]), []
            continue
        first, second, bits = bits[0], bits[1], bits[2:]
        near = swap(x, "slab", first)
        other = swap(x, "slab", second), swap(x, "slab", first | second)
        x = (x + near) + (other[0] + other[1])
    return x, after


def over_angles(x):
    angles = lax.axis_size("angle")
    for b in range(2, angles.bit_length() - 1):
        x = x + swap(x, "angle", 1 << b)
    return [x] + [swap(x, "angle", bit) for bit in ORDER]


def local(projector, block_vox, block_slot, send_ray, block_count, prior, sinogram):
    slabs = lax.axis_size("slab")
    capacity = send_ray.shape[1] // slabs
    ray_dev = sinogram.shape[0]
    vox_dev = prior.shape[0]
    blocks = projector.shape[0]
    half = slabs * ray_dev // 2
    params = pltpu.CompilerParams(vmem_limit_bytes=8 * 1024 * 1024)
    vmem = lambda rows, dtype=F32: pltpu.VMEM((rows, BLK), dtype)
    line = pltpu.VMEM((1, blocks), jnp.int32)
    arguments = (
        projector, block_vox.reshape(1, blocks), block_slot.reshape(1, blocks), send_ray,
        block_count.reshape(1, 1), prior, sinogram,
    )

    proj, vox, rows, volume, sino, mine, theirs = pl.pallas_call(
        first_forward(slabs, capacity, ray_dev),
        out_shape=(
            pltpu.VMEM(projector.shape, BF16), line, line, vmem(vox_dev), vmem(ray_dev),
            vmem(2 * half), vmem(2 * half),
        ),
        in_specs=[whole(pl.ANY)] * 7,
        out_specs=(whole(),) * 7,
        scratch_shapes=[
            line,
            pltpu.VMEM(send_ray.shape, jnp.int32),
            pltpu.VMEM((1, 1), jnp.int32),
            pltpu.SemaphoreType.DMA((2 * CHUNKS,)),
            pltpu.SemaphoreType.DMA((6,)),
        ],
        compiler_params=params,
        name="first_forward",
    )(*[x if x.size == 1 else pltpu.with_memory_space_constraint(x, pltpu.HBM) for x in arguments])
    from_rays, to_rays, from_vox, to_vox, col_total = pl.pallas_call(
        name_places,
        out_shape=(
            pltpu.VMEM((blocks, 2 * half), BF16), pltpu.VMEM((2 * half, blocks), BF16),
            pltpu.VMEM((blocks, vox_dev), BF16), pltpu.VMEM((vox_dev, blocks), BF16), vmem(vox_dev),
        ),
        in_specs=[whole()] * 3,
        out_specs=(whole(),) * 5,
        compiler_params=params,
        cost_estimate=pl.CostEstimate(flops=0, bytes_accessed=1 << 20, transcendentals=0),
        name="name_places",
    )(proj, rows, vox)
    turned = pl.pallas_call(
        turn_blocks,
        out_shape=pltpu.VMEM(projector.shape, BF16),
        in_specs=[whole()],
        out_specs=whole(),
        compiler_params=params,
        cost_estimate=pl.CostEstimate(flops=0, bytes_accessed=2 * projector.size * 2, transcendentals=0),
        name="turn_blocks",
    )(proj)
    sums, _ = over_slabs(mine, theirs)
    row_weight = 1.0 / jnp.maximum(sums[half:], 1.0)
    weighted = (row_weight * sums[:half]).astype(BF16)

    corr = pl.pallas_call(
        first_backward,
        out_shape=vmem(2 * vox_dev),
        in_specs=[whole()] * 6,
        out_specs=whole(),
        compiler_params=params,
        name="first_backward",
    )(proj, from_rays, to_vox, weighted, swap(weighted, "slab", 1), col_total)

    volume, col_weight, mine, theirs = pl.pallas_call(
        next_forward(ray_dev),
        out_shape=(vmem(vox_dev), vmem(vox_dev), vmem(half), vmem(half)),
        in_specs=[whole()] * 9,
        out_specs=(whole(),) * 4,
        compiler_params=params,
        name="next_forward",
    )(turned, from_vox, to_rays, volume, *over_angles(corr), sino)
    residual, projector = over_slabs(mine, theirs, projector)
    count = blocks * 3 // 4
    fetched = [
        pl.pallas_call(
            fetch_blocks(low),
            out_shape=pltpu.VMEM((size,) + projector.shape[1:], BF16),
            in_specs=[whole(pl.ANY)],
            out_specs=whole(),
            scratch_shapes=[pltpu.SemaphoreType.DMA],
            compiler_params=params,
            cost_estimate=pl.CostEstimate(flops=0, bytes_accessed=size << 16, transcendentals=0),
            name="fetch_blocks",
        )(pltpu.with_memory_space_constraint(projector, pltpu.HBM))
        for low, size in ((0, count), (count, blocks - count))
    ]
    early, late = fetched
    residual, early = lax.optimization_barrier((residual, early))
    residual = row_weight * residual
    weighted = residual.astype(BF16)
    start = lax.div(lax.axis_index("slab"), 2) * ray_dev
    residual = lax.dynamic_slice_in_dim(residual, start, ray_dev)

    corr = pl.pallas_call(
        last_to_voxels,
        out_shape=vmem(vox_dev),
        in_specs=[whole()] * 6,
        out_specs=whole(),
        compiler_params=params,
        name="last_backward",
    )(early, late, from_rays, to_vox, weighted, swap(weighted, "slab", 1))
    volume = pl.pallas_call(
        last_update,
        out_shape=jax.ShapeDtypeStruct((vox_dev, BLK), F32),
        in_specs=[whole()] * 6,
        out_specs=whole(),
        compiler_params=params,
        name="last_update",
    )(volume, col_weight, *over_angles(corr))
    return volume, residual


def solution(mesh):
    return jax.shard_map(
        local,
        mesh=mesh,
        in_specs=(
            P(("slab", "angle"), None, None),
            P(("slab", "angle")),
            P(("slab", "angle")),
            P(("slab", "angle"), None),
            P(("slab", "angle")),
            P("slab", None),
            P(("slab", "angle"), None),
        ),
        out_specs=(P("slab", None), P(("slab", "angle"), None)),
        check_vma=False,
    )
```

```python
import jax
import jax.numpy as jnp
from jax import lax
from jax.experimental import pallas as pl
from jax.experimental.pallas import tpu as pltpu
from jax.sharding import PartitionSpec as P

ITERS = 2
F32 = jnp.float32
BF16 = jnp.bfloat16
BLK = 128
CHUNKS = 2
ORDER = (1, 2, 3)


def whole(space=pltpu.VMEM):
    return pl.BlockSpec(memory_space=space)


def iota(shape, dim):
    return lax.broadcasted_iota(jnp.int32, shape, dim)


def split3(x):
    hi = x.astype(BF16)
    rest = x - hi.astype(F32)
    mid = rest.astype(BF16)
    low = (rest - mid.astype(F32)).astype(BF16)
    return hi, mid, low


def dot(a, b, dims=((1,), (0,))):
    return lax.dot_general(a, b, (dims, ((), ())), preferred_element_type=F32)


def one_hot_t(row, size):
    return jnp.where(iota((size, row.shape[1]), 0) == row, 1.0, 0.0)


def block_rows(slot, ray, count, slabs, capacity, ray_dev):
    slots = ray.shape[1]
    picks = one_hot_t(slot, slots).astype(BF16)
    rays = jnp.broadcast_to(ray, (16, slots)).astype(F32).astype(BF16)
    ray = dot(rays, picks)[0:1, :].astype(jnp.int32)
    owner = jnp.zeros_like(slot)
    for o in range(1, slabs):
        owner = owner + jnp.where(slot >= o * capacity, 1, 0)
    place = (owner & 1) * (slabs // 2) + (owner >> 1)
    stored = iota(slot.shape, 1) < count
    return jnp.where(stored, place * ray_dev + ray, -1)


def products(proj, vectors, sums=False, before=None, turn=False):
    blocks = proj.shape[0]
    group = 16
    row = iota((group, BLK), 0)
    tops, lows = [], []
    for g in range(blocks // group):
        if before is not None:
            before(g * group)
        mine = vectors[g * group:(g + 1) * group]
        left = jnp.concatenate([jnp.where(row == c, mine, 0.0) for c in range(group)], 1)
        if sums:
            ones = jnp.concatenate([jnp.where(row == c, 1.0, 0.0) for c in range(group)], 1)
            left = jnp.concatenate([left, ones], 0)
        if turn:
            right = jnp.concatenate([proj[k].T for k in range(g * group, (g + 1) * group)], 0)
        else:
            right = proj[g * group:(g + 1) * group].reshape(group * BLK, BLK)
        out = dot(left.astype(BF16), right)
        tops.append(out[:group])
        if sums:
            lows.append(out[group:])
    columns = jnp.concatenate(tops, 0)
    return jnp.concatenate([columns, jnp.concatenate(lows, 0)], 1) if sums else columns


def collect(places, columns):
    return dot(jnp.concatenate([places] * 3, 1), jnp.concatenate(split3(columns), 0))


def backward(proj, weighted, picks, places):
    return collect(places, products(proj, dot(picks, weighted)))


def forward_turned(turned, volume, picks, places):
    return collect(places, products(turned, dot(picks, volume.astype(BF16))))


def name_places(proj, rows, vox, from_rays, to_rays, from_vox, to_vox, columns):
    spots = one_hot_t(rows[...], to_rays.shape[0])
    from_rays[...] = spots.T.astype(BF16)
    to_rays[...] = spots.astype(BF16)
    spots = one_hot_t(vox[...], to_vox.shape[0])
    from_vox[...] = spots.T.astype(BF16)
    places = (spots * jnp.where(rows[...] >= 0, 1.0, 0.0)).astype(BF16)
    to_vox[...] = places
    columns[...] = collect(places, products(proj, jnp.ones((proj.shape[0], BLK), F32)))


def turn_blocks(proj, turned):
    for k in range(proj.shape[0]):
        turned[k] = proj[k].T


def last_to_voxels(early, late, picks, places, mine, theirs, corr):
    picked = dot(picks[...], join_halves(mine, theirs))
    count = early.shape[0]
    columns = [products(early, picked[:count]), products(late, picked[count:])]
    corr[...] = collect(places[...], jnp.concatenate(columns, 0))


def last_update(volume, weight, corr, near, mid, far, out):
    out[...] = volume[...] + weight[...] * ((corr[...] + near[...]) + (mid[...] + far[...]))


def fetch_blocks(start):
    def kernel(proj_hbm, proj, sem):
        copy = pltpu.make_async_copy(proj_hbm.at[pl.ds(start, proj.shape[0])], proj, sem)
        copy.start()
        copy.wait()

    return kernel


def put_partial(sums, sino, mine, theirs, ray_dev):
    half = sums.shape[0] // 2
    slab = lax.axis_index("slab")
    core = lax.rem(slab, 2)
    top, low = sums[:half], sums[half:]
    mine[0:half, :] = -jnp.where(core == 0, top, low)
    theirs[0:half, :] = -jnp.where(core == 0, low, top)
    at = pl.ds(pl.multiple_of((slab >> 1) * ray_dev, 8), ray_dev)
    mine[at, :] = mine[at, :] + sino


def first_forward(slabs, capacity, ray_dev):
    def kernel(proj_hbm, vox_hbm, slot_hbm, ray_hbm, count_hbm, prior_hbm, sino_hbm,
               proj, vox, rows_out, prior, sino, mine, theirs, slot, ray, count, sems, small):
        blocks = proj_hbm.shape[0]
        half = blocks // 2
        per = half // CHUNKS
        smalls = [
            pltpu.make_async_copy(source, target, small.at[i])
            for i, (source, target) in enumerate([
                (vox_hbm, vox), (slot_hbm, slot), (ray_hbm, ray), (count_hbm, count),
                (prior_hbm, prior), (sino_hbm, sino),
            ])
        ]
        copies = []
        size = blocks // CHUNKS
        for c in range(CHUNKS):
            at = pl.ds(c * size, size)
            copy = pltpu.make_async_copy(proj_hbm.at[at], proj.at[at], sems.at[c])
            copy.start()
            copies.append(copy)
            if not c:
                for copy in smalls:
                    copy.start()
        for copy in smalls:
            copy.wait()

        def before(k):
            if k % size == 0:
                copies[k // size].wait()

        rows = block_rows(slot[...], ray[...], count[...], slabs, capacity, ray_dev)
        rows_out[...] = rows
        total = slabs * ray_dev
        picks = one_hot_t(vox[...], prior.shape[0]).T.astype(BF16)
        columns = products(proj, dot(picks, prior[...].astype(BF16)), True, before, True)
        both = collect(one_hot_t(rows, total).astype(BF16), columns)
        put_partial(both[:, :BLK], sino[...], mine, theirs, ray_dev)
        sums = both[:, BLK:]
        core = lax.rem(lax.axis_index("slab"), 2)
        top, low = sums[:total // 2], sums[total // 2:]
        mine[total // 2:total, :] = jnp.where(core == 0, top, low)
        theirs[total // 2:total, :] = jnp.where(core == 0, low, top)

    return kernel


def join_halves(mine, theirs):
    core = lax.rem(lax.axis_index("slab"), 2)
    mine, theirs = mine[...], theirs[...]
    return jnp.concatenate([jnp.where(core == 0, mine, theirs), jnp.where(core == 0, theirs, mine)], 0)


def next_forward(ray_dev):
    def kernel(proj, picks, places, volume, col_total, own, near, mid, far, sino, volume_out, weight_out, mine, theirs):
        weights = 1.0 / jnp.maximum(col_total[...], 1.0)
        weight_out[...] = weights
        updated = volume[...] + weights * ((own[...] + near[...]) + (mid[...] + far[...]))
        volume_out[...] = updated
        sums = forward_turned(proj, updated, picks[...], places[...])
        put_partial(sums, sino[...], mine, theirs, ray_dev)

    return kernel


def first_backward(proj, picks, places, mine, theirs, corr):
    corr[...] = backward(proj, join_halves(mine, theirs), picks[...], places[...])


def swap(x, axis, bit):
    size = lax.axis_size(axis)
    return lax.ppermute(x, axis, [(i, i ^ bit) for i in range(size)])


def over_slabs(mine, theirs, after=None):
    slabs = lax.axis_size("slab")
    x = mine + swap(theirs, "slab", 1)
    if after is not None:
        x, after = lax.optimization_barrier((x, after))
    bits = [1 << b for b in range(1, slabs.bit_length() - 1)]
    while bits:
        if len(bits) == 1:
            x, bits = x + swap(x, "slab", bits[0]), []
            continue
        first, second, bits = bits[0], bits[1], bits[2:]
        near = swap(x, "slab", first)
        other = swap(x, "slab", second), swap(x, "slab", first | second)
        x = (x + near) + (other[0] + other[1])
    return x, after


def over_angles(x):
    angles = lax.axis_size("angle")
    for b in range(2, angles.bit_length() - 1):
        x = x + swap(x, "angle", 1 << b)
    return [x] + [swap(x, "angle", bit) for bit in ORDER]


def local(projector, block_vox, block_slot, send_ray, block_count, prior, sinogram):
    slabs = lax.axis_size("slab")
    capacity = send_ray.shape[1] // slabs
    ray_dev = sinogram.shape[0]
    vox_dev = prior.shape[0]
    blocks = projector.shape[0]
    half = slabs * ray_dev // 2
    params = pltpu.CompilerParams(vmem_limit_bytes=8 * 1024 * 1024)
    vmem = lambda rows, dtype=F32: pltpu.VMEM((rows, BLK), dtype)
    line = pltpu.VMEM((1, blocks), jnp.int32)
    arguments = (
        projector, block_vox.reshape(1, blocks), block_slot.reshape(1, blocks), send_ray,
        block_count.reshape(1, 1), prior, sinogram,
    )

    proj, vox, rows, volume, sino, mine, theirs = pl.pallas_call(
        first_forward(slabs, capacity, ray_dev),
        out_shape=(
            pltpu.VMEM(projector.shape, BF16), line, line, vmem(vox_dev), vmem(ray_dev),
            vmem(2 * half), vmem(2 * half),
        ),
        in_specs=[whole(pl.ANY)] * 7,
        out_specs=(whole(),) * 7,
        scratch_shapes=[
            line,
            pltpu.VMEM(send_ray.shape, jnp.int32),
            pltpu.VMEM((1, 1), jnp.int32),
            pltpu.SemaphoreType.DMA((2 * CHUNKS,)),
            pltpu.SemaphoreType.DMA((6,)),
        ],
        compiler_params=params,
        name="first_forward",
    )(*[x if x.size == 1 else pltpu.with_memory_space_constraint(x, pltpu.HBM) for x in arguments])
    from_rays, to_rays, from_vox, to_vox, col_total = pl.pallas_call(
        name_places,
        out_shape=(
            pltpu.VMEM((blocks, 2 * half), BF16), pltpu.VMEM((2 * half, blocks), BF16),
            pltpu.VMEM((blocks, vox_dev), BF16), pltpu.VMEM((vox_dev, blocks), BF16), vmem(vox_dev),
        ),
        in_specs=[whole()] * 3,
        out_specs=(whole(),) * 5,
        compiler_params=params,
        cost_estimate=pl.CostEstimate(flops=0, bytes_accessed=1 << 20, transcendentals=0),
        name="name_places",
    )(proj, rows, vox)
    turned = pl.pallas_call(
        turn_blocks,
        out_shape=pltpu.VMEM(projector.shape, BF16),
        in_specs=[whole()],
        out_specs=whole(),
        compiler_params=params,
        cost_estimate=pl.CostEstimate(flops=0, bytes_accessed=2 * projector.size * 2, transcendentals=0),
        name="turn_blocks",
    )(proj)
    sums, _ = over_slabs(mine, theirs)
    row_weight = 1.0 / jnp.maximum(sums[half:], 1.0)
    weighted = (row_weight * sums[:half]).astype(BF16)
    col_total = col_total + swap(col_total, "angle", 1)

    corr = pl.pallas_call(
        first_backward,
        out_shape=vmem(vox_dev),
        in_specs=[whole()] * 5,
        out_specs=whole(),
        compiler_params=params,
        name="first_backward",
    )(proj, from_rays, to_vox, weighted, swap(weighted, "slab", 1))
    angles = lax.axis_size("angle")
    for b in range(1, angles.bit_length() - 1):
        col_total = col_total + swap(col_total, "angle", 1 << b)

    volume, col_weight, mine, theirs = pl.pallas_call(
        next_forward(ray_dev),
        out_shape=(vmem(vox_dev), vmem(vox_dev), vmem(half), vmem(half)),
        in_specs=[whole()] * 10,
        out_specs=(whole(),) * 4,
        compiler_params=params,
        name="next_forward",
    )(turned, from_vox, to_rays, volume, col_total, *over_angles(corr), sino)
    residual, projector = over_slabs(mine, theirs, projector)
    count = blocks * 3 // 4
    fetched = [
        pl.pallas_call(
            fetch_blocks(low),
            out_shape=pltpu.VMEM((size,) + projector.shape[1:], BF16),
            in_specs=[whole(pl.ANY)],
            out_specs=whole(),
            scratch_shapes=[pltpu.SemaphoreType.DMA],
            compiler_params=params,
            cost_estimate=pl.CostEstimate(flops=0, bytes_accessed=size << 16, transcendentals=0),
            name="fetch_blocks",
        )(pltpu.with_memory_space_constraint(projector, pltpu.HBM))
        for low, size in ((0, count), (count, blocks - count))
    ]
    early, late = fetched
    residual, early = lax.optimization_barrier((residual, early))
    residual = row_weight * residual
    weighted = residual.astype(BF16)
    start = lax.div(lax.axis_index("slab"), 2) * ray_dev
    residual = lax.dynamic_slice_in_dim(residual, start, ray_dev)

    corr = pl.pallas_call(
        last_to_voxels,
        out_shape=vmem(vox_dev),
        in_specs=[whole()] * 6,
        out_specs=whole(),
        compiler_params=params,
        name="last_backward",
    )(early, late, from_rays, to_vox, weighted, swap(weighted, "slab", 1))
    volume = pl.pallas_call(
        last_update,
        out_shape=jax.ShapeDtypeStruct((vox_dev, BLK), F32),
        in_specs=[whole()] * 6,
        out_specs=whole(),
        compiler_params=params,
        name="last_update",
    )(volume, col_weight, *over_angles(corr))
    return volume, residual


def solution(mesh):
    return jax.shard_map(
        local,
        mesh=mesh,
        in_specs=(
            P(("slab", "angle"), None, None),
            P(("slab", "angle")),
            P(("slab", "angle")),
            P(("slab", "angle"), None),
            P(("slab", "angle")),
            P("slab", None),
            P(("slab", "angle"), None),
        ),
        out_specs=(P("slab", None), P(("slab", "angle"), None)),
        check_vma=False,
    )
```

```python
import jax
import jax.numpy as jnp
from jax import lax
from jax.experimental import pallas as pl
from jax.experimental.pallas import tpu as pltpu
from jax.sharding import PartitionSpec as P

ITERS = 2
F32 = jnp.float32
BF16 = jnp.bfloat16
BLK = 128
CHUNKS = 2
ORDER = (1, 2, 3)


def whole(space=pltpu.VMEM):
    return pl.BlockSpec(memory_space=space)


def iota(shape, dim):
    return lax.broadcasted_iota(jnp.int32, shape, dim)


def split3(x):
    hi = x.astype(BF16)
    rest = x - hi.astype(F32)
    mid = rest.astype(BF16)
    low = (rest - mid.astype(F32)).astype(BF16)
    return hi, mid, low


def dot(a, b, dims=((1,), (0,))):
    return lax.dot_general(a, b, (dims, ((), ())), preferred_element_type=F32)


def one_hot_t(row, size):
    return jnp.where(iota((size, row.shape[1]), 0) == row, 1.0, 0.0)


def block_rows(slot, ray, count, slabs, capacity, ray_dev):
    slots = ray.shape[1]
    picks = one_hot_t(slot, slots).astype(BF16)
    rays = jnp.broadcast_to(ray, (16, slots)).astype(F32).astype(BF16)
    ray = dot(rays, picks)[0:1, :].astype(jnp.int32)
    owner = jnp.zeros_like(slot)
    for o in range(1, slabs):
        owner = owner + jnp.where(slot >= o * capacity, 1, 0)
    place = (owner & 1) * (slabs // 2) + (owner >> 1)
    stored = iota(slot.shape, 1) < count
    return jnp.where(stored, place * ray_dev + ray, -1)


def products(proj, vectors, sums=False, before=None, turn=False):
    blocks = proj.shape[0]
    group = 16
    row = iota((group, BLK), 0)
    tops, lows = [], []
    for g in range(blocks // group):
        if before is not None:
            before(g * group)
        mine = vectors[g * group:(g + 1) * group]
        left = jnp.concatenate([jnp.where(row == c, mine, 0.0) for c in range(group)], 1)
        if sums:
            ones = jnp.concatenate([jnp.where(row == c, 1.0, 0.0) for c in range(group)], 1)
            left = jnp.concatenate([left, ones], 0)
        if turn:
            right = jnp.concatenate([proj[k].T for k in range(g * group, (g + 1) * group)], 0)
        else:
            right = proj[g * group:(g + 1) * group].reshape(group * BLK, BLK)
        out = dot(left.astype(BF16), right)
        tops.append(out[:group])
        if sums:
            lows.append(out[group:])
    columns = jnp.concatenate(tops, 0)
    return jnp.concatenate([columns, jnp.concatenate(lows, 0)], 1) if sums else columns


def collect(places, columns):
    return dot(jnp.concatenate([places] * 3, 1), jnp.concatenate(split3(columns), 0))


def backward(proj, weighted, picks, places):
    return collect(places, products(proj, dot(picks, weighted)))


def forward_turned(turned, volume, picks, places):
    return collect(places, products(turned, dot(picks, volume.astype(BF16))))


def name_places(proj, rows, vox, from_rays, to_rays, from_vox, to_vox, columns):
    spots = one_hot_t(rows[...], to_rays.shape[0])
    from_rays[...] = spots.T.astype(BF16)
    to_rays[...] = spots.astype(BF16)
    spots = one_hot_t(vox[...], to_vox.shape[0])
    from_vox[...] = spots.T.astype(BF16)
    places = (spots * jnp.where(rows[...] >= 0, 1.0, 0.0)).astype(BF16)
    to_vox[...] = places
    columns[...] = collect(places, products(proj, jnp.ones((proj.shape[0], BLK), F32)))


def turn_blocks(proj, turned):
    for k in range(proj.shape[0]):
        turned[k] = proj[k].T


def last_to_voxels(early, late, picks, places, mine, theirs, corr):
    picked = dot(picks[...], join_halves(mine, theirs))
    count = early.shape[0]
    columns = [products(early, picked[:count]), products(late, picked[count:])]
    corr[...] = collect(places[...], jnp.concatenate(columns, 0))


def last_update(volume, weight, corr, near, mid, far, out):
    out[...] = volume[...] + weight[...] * ((corr[...] + near[...]) + (mid[...] + far[...]))


def fetch_blocks(start):
    def kernel(proj_hbm, proj, sem):
        copy = pltpu.make_async_copy(proj_hbm.at[pl.ds(start, proj.shape[0])], proj, sem)
        copy.start()
        copy.wait()

    return kernel


def put_partial(sums, sino, mine, theirs, ray_dev):
    half = sums.shape[0] // 2
    slab = lax.axis_index("slab")
    core = lax.rem(slab, 2)
    top, low = sums[:half], sums[half:]
    mine[0:half, :] = -jnp.where(core == 0, top, low)
    theirs[0:half, :] = -jnp.where(core == 0, low, top)
    at = pl.ds(pl.multiple_of((slab >> 1) * ray_dev, 8), ray_dev)
    mine[at, :] = mine[at, :] + sino


def first_forward(slabs, capacity, ray_dev):
    def kernel(proj_hbm, vox_hbm, slot_hbm, ray_hbm, count_hbm, prior_hbm, sino_hbm,
               proj, vox, rows_out, prior, sino, mine, theirs, slot, ray, count, sems, small):
        blocks = proj_hbm.shape[0]
        half = blocks // 2
        per = half // CHUNKS
        smalls = [
            pltpu.make_async_copy(source, target, small.at[i])
            for i, (source, target) in enumerate([
                (vox_hbm, vox), (slot_hbm, slot), (ray_hbm, ray), (count_hbm, count),
                (prior_hbm, prior), (sino_hbm, sino),
            ])
        ]
        copies = []
        size = blocks // CHUNKS
        for c in range(CHUNKS):
            at = pl.ds(c * size, size)
            copy = pltpu.make_async_copy(proj_hbm.at[at], proj.at[at], sems.at[c])
            copy.start()
            copies.append(copy)
            if not c:
                for copy in smalls:
                    copy.start()
        for copy in smalls:
            copy.wait()

        def before(k):
            if k % size == 0:
                copies[k // size].wait()

        rows = block_rows(slot[...], ray[...], count[...], slabs, capacity, ray_dev)
        rows_out[...] = rows
        total = slabs * ray_dev
        picks = one_hot_t(vox[...], prior.shape[0]).T.astype(BF16)
        columns = products(proj, dot(picks, prior[...].astype(BF16)), True, before, True)
        both = collect(one_hot_t(rows, total).astype(BF16), columns)
        put_partial(both[:, :BLK], sino[...], mine, theirs, ray_dev)
        sums = both[:, BLK:]
        core = lax.rem(lax.axis_index("slab"), 2)
        top, low = sums[:total // 2], sums[total // 2:]
        mine[total // 2:total, :] = jnp.where(core == 0, top, low)
        theirs[total // 2:total, :] = jnp.where(core == 0, low, top)

    return kernel


def join_halves(mine, theirs):
    core = lax.rem(lax.axis_index("slab"), 2)
    mine, theirs = mine[...], theirs[...]
    return jnp.concatenate([jnp.where(core == 0, mine, theirs), jnp.where(core == 0, theirs, mine)], 0)


def next_forward(ray_dev):
    def kernel(proj, picks, places, volume, col_total, own, near, mid, far, sino, volume_out, weight_out, mine, theirs):
        weights = 1.0 / jnp.maximum(col_total[...], 1.0)
        weight_out[...] = weights
        updated = volume[...] + weights * ((own[...] + near[...]) + (mid[...] + far[...]))
        volume_out[...] = updated
        sums = forward_turned(proj, updated, picks[...], places[...])
        put_partial(sums, sino[...], mine, theirs, ray_dev)

    return kernel


def first_backward(proj, picks, places, mine, theirs, corr):
    corr[...] = backward(proj, join_halves(mine, theirs), picks[...], places[...])


def swap(x, axis, bit):
    size = lax.axis_size(axis)
    return lax.ppermute(x, axis, [(i, i ^ bit) for i in range(size)])


def over_slabs(mine, theirs, after=None):
    slabs = lax.axis_size("slab")
    x = mine + swap(theirs, "slab", 1)
    if after is not None:
        x, after = lax.optimization_barrier((x, after))
    bits = [1 << b for b in range(1, slabs.bit_length() - 1)]
    while bits:
        if len(bits) == 1:
            x, bits = x + swap(x, "slab", bits[0]), []
            continue
        first, second, bits = bits[0], bits[1], bits[2:]
        near = swap(x, "slab", first)
        other = swap(x, "slab", second), swap(x, "slab", first | second)
        x = (x + near) + (other[0] + other[1])
    return x, after


def over_angles(x):
    angles = lax.axis_size("angle")
    for b in range(2, angles.bit_length() - 1):
        x = x + swap(x, "angle", 1 << b)
    return [x] + [swap(x, "angle", bit) for bit in ORDER]


def local(projector, block_vox, block_slot, send_ray, block_count, prior, sinogram):
    slabs = lax.axis_size("slab")
    capacity = send_ray.shape[1] // slabs
    ray_dev = sinogram.shape[0]
    vox_dev = prior.shape[0]
    blocks = projector.shape[0]
    half = slabs * ray_dev // 2
    params = pltpu.CompilerParams(vmem_limit_bytes=8 * 1024 * 1024)
    vmem = lambda rows, dtype=F32: pltpu.VMEM((rows, BLK), dtype)
    line = pltpu.VMEM((1, blocks), jnp.int32)
    arguments = (
        projector, block_vox.reshape(1, blocks), block_slot.reshape(1, blocks), send_ray,
        block_count.reshape(1, 1), prior, sinogram,
    )

    proj, vox, rows, volume, sino, mine, theirs = pl.pallas_call(
        first_forward(slabs, capacity, ray_dev),
        out_shape=(
            pltpu.VMEM(projector.shape, BF16), line, line, vmem(vox_dev), vmem(ray_dev),
            vmem(2 * half), vmem(2 * half),
        ),
        in_specs=[whole(pl.ANY)] * 7,
        out_specs=(whole(),) * 7,
        scratch_shapes=[
            line,
            pltpu.VMEM(send_ray.shape, jnp.int32),
            pltpu.VMEM((1, 1), jnp.int32),
            pltpu.SemaphoreType.DMA((2 * CHUNKS,)),
            pltpu.SemaphoreType.DMA((6,)),
        ],
        compiler_params=params,
        name="first_forward",
    )(*[x if x.size == 1 else pltpu.with_memory_space_constraint(x, pltpu.HBM) for x in arguments])
    from_rays, to_rays, from_vox, to_vox, col_total = pl.pallas_call(
        name_places,
        out_shape=(
            pltpu.VMEM((blocks, 2 * half), BF16), pltpu.VMEM((2 * half, blocks), BF16),
            pltpu.VMEM((blocks, vox_dev), BF16), pltpu.VMEM((vox_dev, blocks), BF16), vmem(vox_dev),
        ),
        in_specs=[whole()] * 3,
        out_specs=(whole(),) * 5,
        compiler_params=params,
        cost_estimate=pl.CostEstimate(flops=0, bytes_accessed=1 << 20, transcendentals=0),
        name="name_places",
    )(proj, rows, vox)
    turned = pl.pallas_call(
        turn_blocks,
        out_shape=pltpu.VMEM(projector.shape, BF16),
        in_specs=[whole()],
        out_specs=whole(),
        compiler_params=params,
        cost_estimate=pl.CostEstimate(flops=0, bytes_accessed=2 * projector.size * 2, transcendentals=0),
        name="turn_blocks",
    )(proj)
    sums, _ = over_slabs(mine, theirs)
    row_weight = 1.0 / jnp.maximum(sums[half:], 1.0)
    weighted = (row_weight * sums[:half]).astype(BF16)
    angles = lax.axis_size("angle")
    for b in reversed(range(1, angles.bit_length() - 1)):
        col_total = col_total + swap(col_total, "angle", 1 << b)

    corr = pl.pallas_call(
        first_backward,
        out_shape=vmem(vox_dev),
        in_specs=[whole()] * 5,
        out_specs=whole(),
        compiler_params=params,
        name="first_backward",
    )(proj, from_rays, to_vox, weighted, swap(weighted, "slab", 1))
    col_total = col_total + swap(col_total, "angle", 1)

    volume, col_weight, mine, theirs = pl.pallas_call(
        next_forward(ray_dev),
        out_shape=(vmem(vox_dev), vmem(vox_dev), vmem(half), vmem(half)),
        in_specs=[whole()] * 10,
        out_specs=(whole(),) * 4,
        compiler_params=params,
        name="next_forward",
    )(turned, from_vox, to_rays, volume, col_total, *over_angles(corr), sino)
    residual, projector = over_slabs(mine, theirs, projector)
    count = blocks * 3 // 4
    fetched = [
        pl.pallas_call(
            fetch_blocks(low),
            out_shape=pltpu.VMEM((size,) + projector.shape[1:], BF16),
            in_specs=[whole(pl.ANY)],
            out_specs=whole(),
            scratch_shapes=[pltpu.SemaphoreType.DMA],
            compiler_params=params,
            cost_estimate=pl.CostEstimate(flops=0, bytes_accessed=size << 16, transcendentals=0),
            name="fetch_blocks",
        )(pltpu.with_memory_space_constraint(projector, pltpu.HBM))
        for low, size in ((0, count), (count, blocks - count))
    ]
    early, late = fetched
    residual, early = lax.optimization_barrier((residual, early))
    residual = row_weight * residual
    weighted = residual.astype(BF16)
    start = lax.div(lax.axis_index("slab"), 2) * ray_dev
    residual = lax.dynamic_slice_in_dim(residual, start, ray_dev)

    corr = pl.pallas_call(
        last_to_voxels,
        out_shape=vmem(vox_dev),
        in_specs=[whole()] * 6,
        out_specs=whole(),
        compiler_params=params,
        name="last_backward",
    )(early, late, from_rays, to_vox, weighted, swap(weighted, "slab", 1))
    volume = pl.pallas_call(
        last_update,
        out_shape=jax.ShapeDtypeStruct((vox_dev, BLK), F32),
        in_specs=[whole()] * 6,
        out_specs=whole(),
        compiler_params=params,
        name="last_update",
    )(volume, col_weight, *over_angles(corr))
    return volume, residual


def solution(mesh):
    return jax.shard_map(
        local,
        mesh=mesh,
        in_specs=(
            P(("slab", "angle"), None, None),
            P(("slab", "angle")),
            P(("slab", "angle")),
            P(("slab", "angle"), None),
            P(("slab", "angle")),
            P("slab", None),
            P(("slab", "angle"), None),
        ),
        out_specs=(P("slab", None), P(("slab", "angle"), None)),
        check_vma=False,
    )
```

```python
import jax
import jax.numpy as jnp
from jax import lax
from jax.experimental import pallas as pl
from jax.experimental.pallas import tpu as pltpu
from jax.sharding import PartitionSpec as P

ITERS = 2
F32 = jnp.float32
BF16 = jnp.bfloat16
BLK = 128
CHUNKS = 2
ORDER = (1, 2, 3)


def whole(space=pltpu.VMEM):
    return pl.BlockSpec(memory_space=space)


def iota(shape, dim):
    return lax.broadcasted_iota(jnp.int32, shape, dim)


def split3(x):
    hi = x.astype(BF16)
    rest = x - hi.astype(F32)
    mid = rest.astype(BF16)
    low = (rest - mid.astype(F32)).astype(BF16)
    return hi, mid, low


def dot(a, b, dims=((1,), (0,))):
    return lax.dot_general(a, b, (dims, ((), ())), preferred_element_type=F32)


def one_hot_t(row, size):
    return jnp.where(iota((size, row.shape[1]), 0) == row, 1.0, 0.0)


def block_rows(slot, ray, count, slabs, capacity, ray_dev):
    slots = ray.shape[1]
    picks = one_hot_t(slot, slots).astype(BF16)
    rays = jnp.broadcast_to(ray, (16, slots)).astype(F32).astype(BF16)
    ray = dot(rays, picks)[0:1, :].astype(jnp.int32)
    owner = jnp.zeros_like(slot)
    for o in range(1, slabs):
        owner = owner + jnp.where(slot >= o * capacity, 1, 0)
    place = (owner & 1) * (slabs // 2) + (owner >> 1)
    stored = iota(slot.shape, 1) < count
    return jnp.where(stored, place * ray_dev + ray, -1)


def products(proj, vectors, sums=False, before=None, turn=False):
    blocks = proj.shape[0]
    group = 16
    row = iota((group, BLK), 0)
    tops, lows = [], []
    for g in range(blocks // group):
        if before is not None:
            before(g * group)
        mine = vectors[g * group:(g + 1) * group]
        left = jnp.concatenate([jnp.where(row == c, mine, 0.0) for c in range(group)], 1)
        if sums:
            ones = jnp.concatenate([jnp.where(row == c, 1.0, 0.0) for c in range(group)], 1)
            left = jnp.concatenate([left, ones], 0)
        if turn:
            right = jnp.concatenate([proj[k].T for k in range(g * group, (g + 1) * group)], 0)
        else:
            right = proj[g * group:(g + 1) * group].reshape(group * BLK, BLK)
        out = dot(left.astype(BF16), right)
        tops.append(out[:group])
        if sums:
            lows.append(out[group:])
    columns = jnp.concatenate(tops, 0)
    return jnp.concatenate([columns, jnp.concatenate(lows, 0)], 1) if sums else columns


def collect(places, columns):
    return dot(jnp.concatenate([places] * 3, 1), jnp.concatenate(split3(columns), 0))


def backward(proj, weighted, picks, places):
    return collect(places, products(proj, dot(picks, weighted)))


def forward_turned(turned, volume, picks, places):
    return collect(places, products(turned, dot(picks, volume.astype(BF16))))


def name_places(proj, rows, vox, from_rays, to_rays, from_vox, to_vox, columns):
    spots = one_hot_t(rows[...], to_rays.shape[0])
    from_rays[...] = spots.T.astype(BF16)
    to_rays[...] = spots.astype(BF16)
    spots = one_hot_t(vox[...], to_vox.shape[0])
    from_vox[...] = spots.T.astype(BF16)
    places = (spots * jnp.where(rows[...] >= 0, 1.0, 0.0)).astype(BF16)
    to_vox[...] = places
    columns[...] = collect(places, products(proj, jnp.ones((proj.shape[0], BLK), F32)))


def turn_blocks(proj, turned):
    for k in range(proj.shape[0]):
        turned[k] = proj[k].T


def last_to_voxels(early, late, picks, places, mine, theirs, corr):
    picked = dot(picks[...], join_halves(mine, theirs))
    count = early.shape[0]
    columns = [products(early, picked[:count]), products(late, picked[count:])]
    corr[...] = collect(places[...], jnp.concatenate(columns, 0))


def last_update(volume, weight, corr, near, mid, far, out):
    out[...] = volume[...] + weight[...] * ((corr[...] + near[...]) + (mid[...] + far[...]))


def fetch_blocks(start):
    def kernel(proj_hbm, proj, sem):
        copy = pltpu.make_async_copy(proj_hbm.at[pl.ds(start, proj.shape[0])], proj, sem)
        copy.start()
        copy.wait()

    return kernel


def put_partial(sums, sino, mine, theirs, ray_dev):
    half = sums.shape[0] // 2
    slab = lax.axis_index("slab")
    core = lax.rem(slab, 2)
    top, low = sums[:half], sums[half:]
    mine[0:half, :] = -jnp.where(core == 0, top, low)
    theirs[0:half, :] = -jnp.where(core == 0, low, top)
    at = pl.ds(pl.multiple_of((slab >> 1) * ray_dev, 8), ray_dev)
    mine[at, :] = mine[at, :] + sino


def first_forward(slabs, capacity, ray_dev):
    def kernel(proj_hbm, vox_hbm, slot_hbm, ray_hbm, count_hbm, prior_hbm, sino_hbm,
               proj, vox, rows_out, prior, sino, mine, theirs, slot, ray, count, sems, small):
        blocks = proj_hbm.shape[0]
        half = blocks // 2
        per = half // CHUNKS
        smalls = [
            pltpu.make_async_copy(source, target, small.at[i])
            for i, (source, target) in enumerate([
                (vox_hbm, vox), (slot_hbm, slot), (ray_hbm, ray), (count_hbm, count),
                (prior_hbm, prior), (sino_hbm, sino),
            ])
        ]
        copies = []
        size = blocks // CHUNKS
        for c in range(CHUNKS):
            at = pl.ds(c * size, size)
            copy = pltpu.make_async_copy(proj_hbm.at[at], proj.at[at], sems.at[c])
            copy.start()
            copies.append(copy)
            if not c:
                for copy in smalls:
                    copy.start()
        for copy in smalls:
            copy.wait()

        def before(k):
            if k % size == 0:
                copies[k // size].wait()

        rows = block_rows(slot[...], ray[...], count[...], slabs, capacity, ray_dev)
        rows_out[...] = rows
        total = slabs * ray_dev
        picks = one_hot_t(vox[...], prior.shape[0]).T.astype(BF16)
        columns = products(proj, dot(picks, prior[...].astype(BF16)), True, before, True)
        both = collect(one_hot_t(rows, total).astype(BF16), columns)
        put_partial(both[:, :BLK], sino[...], mine, theirs, ray_dev)
        sums = both[:, BLK:]
        core = lax.rem(lax.axis_index("slab"), 2)
        top, low = sums[:total // 2], sums[total // 2:]
        mine[total // 2:total, :] = jnp.where(core == 0, top, low)
        theirs[total // 2:total, :] = jnp.where(core == 0, low, top)

    return kernel


def join_halves(mine, theirs):
    core = lax.rem(lax.axis_index("slab"), 2)
    mine, theirs = mine[...], theirs[...]
    return jnp.concatenate([jnp.where(core == 0, mine, theirs), jnp.where(core == 0, theirs, mine)], 0)


def next_forward(ray_dev):
    def kernel(proj, picks, places, volume, col_total, own, near, mid, far, sino, volume_out, weight_out, mine, theirs):
        weights = 1.0 / jnp.maximum(col_total[...], 1.0)
        weight_out[...] = weights
        updated = volume[...] + weights * ((own[...] + near[...]) + (mid[...] + far[...]))
        volume_out[...] = updated
        sums = forward_turned(proj, updated, picks[...], places[...])
        put_partial(sums, sino[...], mine, theirs, ray_dev)

    return kernel


def first_backward(proj, picks, places, mine, theirs, corr):
    corr[...] = backward(proj, join_halves(mine, theirs), picks[...], places[...])


def swap(x, axis, bit):
    size = lax.axis_size(axis)
    return lax.ppermute(x, axis, [(i, i ^ bit) for i in range(size)])


def over_slabs(mine, theirs, after=None):
    slabs = lax.axis_size("slab")
    x = mine + swap(theirs, "slab", 1)
    if after is not None:
        x, after = lax.optimization_barrier((x, after))
    bits = [1 << b for b in range(1, slabs.bit_length() - 1)]
    while bits:
        if len(bits) == 1:
            x, bits = x + swap(x, "slab", bits[0]), []
            continue
        first, second, bits = bits[0], bits[1], bits[2:]
        far = swap(x, "slab", first | second)
        x = (x + swap(x, "slab", first)) + (swap(x, "slab", second) + far)
    return x, after


def over_angles(x):
    angles = lax.axis_size("angle")
    for b in range(2, angles.bit_length() - 1):
        x = x + swap(x, "angle", 1 << b)
    return [x] + [swap(x, "angle", bit) for bit in ORDER]


def local(projector, block_vox, block_slot, send_ray, block_count, prior, sinogram):
    slabs = lax.axis_size("slab")
    capacity = send_ray.shape[1] // slabs
    ray_dev = sinogram.shape[0]
    vox_dev = prior.shape[0]
    blocks = projector.shape[0]
    half = slabs * ray_dev // 2
    params = pltpu.CompilerParams(vmem_limit_bytes=8 * 1024 * 1024)
    vmem = lambda rows, dtype=F32: pltpu.VMEM((rows, BLK), dtype)
    line = pltpu.VMEM((1, blocks), jnp.int32)
    arguments = (
        projector, block_vox.reshape(1, blocks), block_slot.reshape(1, blocks), send_ray,
        block_count.reshape(1, 1), prior, sinogram,
    )

    proj, vox, rows, volume, sino, mine, theirs = pl.pallas_call(
        first_forward(slabs, capacity, ray_dev),
        out_shape=(
            pltpu.VMEM(projector.shape, BF16), line, line, vmem(vox_dev), vmem(ray_dev),
            vmem(2 * half), vmem(2 * half),
        ),
        in_specs=[whole(pl.ANY)] * 7,
        out_specs=(whole(),) * 7,
        scratch_shapes=[
            line,
            pltpu.VMEM(send_ray.shape, jnp.int32),
            pltpu.VMEM((1, 1), jnp.int32),
            pltpu.SemaphoreType.DMA((2 * CHUNKS,)),
            pltpu.SemaphoreType.DMA((6,)),
        ],
        compiler_params=params,
        name="first_forward",
    )(*[x if x.size == 1 else pltpu.with_memory_space_constraint(x, pltpu.HBM) for x in arguments])
    from_rays, to_rays, from_vox, to_vox, col_total = pl.pallas_call(
        name_places,
        out_shape=(
            pltpu.VMEM((blocks, 2 * half), BF16), pltpu.VMEM((2 * half, blocks), BF16),
            pltpu.VMEM((blocks, vox_dev), BF16), pltpu.VMEM((vox_dev, blocks), BF16), vmem(vox_dev),
        ),
        in_specs=[whole()] * 3,
        out_specs=(whole(),) * 5,
        compiler_params=params,
        cost_estimate=pl.CostEstimate(flops=0, bytes_accessed=1 << 20, transcendentals=0),
        name="name_places",
    )(proj, rows, vox)
    turned = pl.pallas_call(
        turn_blocks,
        out_shape=pltpu.VMEM(projector.shape, BF16),
        in_specs=[whole()],
        out_specs=whole(),
        compiler_params=params,
        cost_estimate=pl.CostEstimate(flops=0, bytes_accessed=2 * projector.size * 2, transcendentals=0),
        name="turn_blocks",
    )(proj)
    sums, _ = over_slabs(mine, theirs)
    row_weight = 1.0 / jnp.maximum(sums[half:], 1.0)
    weighted = (row_weight * sums[:half]).astype(BF16)
    angles = lax.axis_size("angle")
    for b in reversed(range(1, angles.bit_length() - 1)):
        col_total = col_total + swap(col_total, "angle", 1 << b)

    corr = pl.pallas_call(
        first_backward,
        out_shape=vmem(vox_dev),
        in_specs=[whole()] * 5,
        out_specs=whole(),
        compiler_params=params,
        name="first_backward",
    )(proj, from_rays, to_vox, weighted, swap(weighted, "slab", 1))
    col_total = col_total + swap(col_total, "angle", 1)

    volume, col_weight, mine, theirs = pl.pallas_call(
        next_forward(ray_dev),
        out_shape=(vmem(vox_dev), vmem(vox_dev), vmem(half), vmem(half)),
        in_specs=[whole()] * 10,
        out_specs=(whole(),) * 4,
        compiler_params=params,
        name="next_forward",
    )(turned, from_vox, to_rays, volume, col_total, *over_angles(corr), sino)
    residual, projector = over_slabs(mine, theirs, projector)
    count = blocks * 3 // 4
    fetched = [
        pl.pallas_call(
            fetch_blocks(low),
            out_shape=pltpu.VMEM((size,) + projector.shape[1:], BF16),
            in_specs=[whole(pl.ANY)],
            out_specs=whole(),
            scratch_shapes=[pltpu.SemaphoreType.DMA],
            compiler_params=params,
            cost_estimate=pl.CostEstimate(flops=0, bytes_accessed=size << 16, transcendentals=0),
            name="fetch_blocks",
        )(pltpu.with_memory_space_constraint(projector, pltpu.HBM))
        for low, size in ((0, count), (count, blocks - count))
    ]
    early, late = fetched
    residual, early = lax.optimization_barrier((residual, early))
    residual = row_weight * residual
    weighted = residual.astype(BF16)
    start = lax.div(lax.axis_index("slab"), 2) * ray_dev
    residual = lax.dynamic_slice_in_dim(residual, start, ray_dev)

    corr = pl.pallas_call(
        last_to_voxels,
        out_shape=vmem(vox_dev),
        in_specs=[whole()] * 6,
        out_specs=whole(),
        compiler_params=params,
        name="last_backward",
    )(early, late, from_rays, to_vox, weighted, swap(weighted, "slab", 1))
    volume = pl.pallas_call(
        last_update,
        out_shape=jax.ShapeDtypeStruct((vox_dev, BLK), F32),
        in_specs=[whole()] * 6,
        out_specs=whole(),
        compiler_params=params,
        name="last_update",
    )(volume, col_weight, *over_angles(corr))
    return volume, residual


def solution(mesh):
    return jax.shard_map(
        local,
        mesh=mesh,
        in_specs=(
            P(("slab", "angle"), None, None),
            P(("slab", "angle")),
            P(("slab", "angle")),
            P(("slab", "angle"), None),
            P(("slab", "angle")),
            P("slab", None),
            P(("slab", "angle"), None),
        ),
        out_specs=(P("slab", None), P(("slab", "angle"), None)),
        check_vma=False,
    )
```

```python
import jax
import jax.numpy as jnp
from jax import lax
from jax.experimental import pallas as pl
from jax.experimental.pallas import tpu as pltpu
from jax.sharding import PartitionSpec as P

ITERS = 2
F32 = jnp.float32
BF16 = jnp.bfloat16
BLK = 128
CHUNKS = 2
ORDER = (1, 2, 3)


def whole(space=pltpu.VMEM):
    return pl.BlockSpec(memory_space=space)


def iota(shape, dim):
    return lax.broadcasted_iota(jnp.int32, shape, dim)


def split3(x):
    hi = x.astype(BF16)
    rest = x - hi.astype(F32)
    mid = rest.astype(BF16)
    low = (rest - mid.astype(F32)).astype(BF16)
    return hi, mid, low


def dot(a, b, dims=((1,), (0,))):
    return lax.dot_general(a, b, (dims, ((), ())), preferred_element_type=F32)


def one_hot_t(row, size):
    return jnp.where(iota((size, row.shape[1]), 0) == row, 1.0, 0.0)


def block_rows(slot, ray, count, slabs, capacity, ray_dev):
    slots = ray.shape[1]
    picks = one_hot_t(slot, slots).astype(BF16)
    rays = jnp.broadcast_to(ray, (16, slots)).astype(F32).astype(BF16)
    ray = dot(rays, picks)[0:1, :].astype(jnp.int32)
    owner = jnp.zeros_like(slot)
    for o in range(1, slabs):
        owner = owner + jnp.where(slot >= o * capacity, 1, 0)
    place = (owner & 1) * (slabs // 2) + (owner >> 1)
    stored = iota(slot.shape, 1) < count
    return jnp.where(stored, place * ray_dev + ray, -1)


def products(proj, vectors, sums=False, before=None, turn=False):
    blocks = proj.shape[0]
    group = 16
    row = iota((group, BLK), 0)
    tops, lows = [], []
    for g in range(blocks // group):
        if before is not None:
            before(g * group)
        mine = vectors[g * group:(g + 1) * group]
        left = jnp.concatenate([jnp.where(row == c, mine, 0.0) for c in range(group)], 1)
        if sums:
            ones = jnp.concatenate([jnp.where(row == c, 1.0, 0.0) for c in range(group)], 1)
            left = jnp.concatenate([left, ones], 0)
        if turn:
            right = jnp.concatenate([proj[k].T for k in range(g * group, (g + 1) * group)], 0)
        else:
            right = proj[g * group:(g + 1) * group].reshape(group * BLK, BLK)
        out = dot(left.astype(BF16), right)
        tops.append(out[:group])
        if sums:
            lows.append(out[group:])
    columns = jnp.concatenate(tops, 0)
    return jnp.concatenate([columns, jnp.concatenate(lows, 0)], 1) if sums else columns


def collect(places, columns):
    return dot(jnp.concatenate([places] * 3, 1), jnp.concatenate(split3(columns), 0))


def backward(proj, weighted, picks, places):
    return collect(places, products(proj, dot(picks, weighted)))


def forward_turned(turned, volume, picks, places):
    return collect(places, products(turned, dot(picks, volume.astype(BF16))))


def name_places(proj, rows, vox, from_rays, to_rays, from_vox, to_vox, columns):
    spots = one_hot_t(rows[...], to_rays.shape[0])
    from_rays[...] = spots.T.astype(BF16)
    to_rays[...] = spots.astype(BF16)
    spots = one_hot_t(vox[...], to_vox.shape[0])
    from_vox[...] = spots.T.astype(BF16)
    places = (spots * jnp.where(rows[...] >= 0, 1.0, 0.0)).astype(BF16)
    to_vox[...] = places
    columns[...] = collect(places, products(proj, jnp.ones((proj.shape[0], BLK), F32)))


def turn_blocks(proj, turned):
    for k in range(proj.shape[0]):
        turned[k] = proj[k].T


def last_to_voxels(early, late, picks, places, mine, theirs, corr):
    picked = dot(picks[...], join_halves(mine, theirs))
    count = early.shape[0]
    columns = [products(early, picked[:count]), products(late, picked[count:])]
    corr[...] = collect(places[...], jnp.concatenate(columns, 0))


def last_update(volume, weight, corr, near, mid, far, out):
    out[...] = volume[...] + weight[...] * ((corr[...] + near[...]) + (mid[...] + far[...]))


def fetch_blocks(start):
    def kernel(proj_hbm, proj, sem):
        copy = pltpu.make_async_copy(proj_hbm.at[pl.ds(start, proj.shape[0])], proj, sem)
        copy.start()
        copy.wait()

    return kernel


def put_partial(sums, sino, mine, theirs, ray_dev):
    half = sums.shape[0] // 2
    slab = lax.axis_index("slab")
    core = lax.rem(slab, 2)
    top, low = sums[:half], sums[half:]
    mine[0:half, :] = -jnp.where(core == 0, top, low)
    theirs[0:half, :] = -jnp.where(core == 0, low, top)
    at = pl.ds(pl.multiple_of((slab >> 1) * ray_dev, 8), ray_dev)
    mine[at, :] = mine[at, :] + sino


def first_forward(slabs, capacity, ray_dev):
    def kernel(proj_hbm, vox_hbm, slot_hbm, ray_hbm, count_hbm, prior_hbm, sino_hbm,
               proj, vox, rows_out, prior, sino, mine, theirs, slot, ray, count, sems, small):
        blocks = proj_hbm.shape[0]
        half = blocks // 2
        per = half // CHUNKS
        smalls = [
            pltpu.make_async_copy(source, target, small.at[i])
            for i, (source, target) in enumerate([
                (vox_hbm, vox), (slot_hbm, slot), (ray_hbm, ray), (count_hbm, count),
                (prior_hbm, prior), (sino_hbm, sino),
            ])
        ]
        copies = []
        size = blocks // CHUNKS
        for c in range(CHUNKS):
            at = pl.ds(c * size, size)
            copy = pltpu.make_async_copy(proj_hbm.at[at], proj.at[at], sems.at[c])
            copy.start()
            copies.append(copy)
            if not c:
                for copy in smalls:
                    copy.start()
        for copy in smalls:
            copy.wait()

        def before(k):
            if k % size == 0:
                copies[k // size].wait()

        rows = block_rows(slot[...], ray[...], count[...], slabs, capacity, ray_dev)
        rows_out[...] = rows
        total = slabs * ray_dev
        picks = one_hot_t(vox[...], prior.shape[0]).T.astype(BF16)
        columns = products(proj, dot(picks, prior[...].astype(BF16)), True, before, True)
        both = collect(one_hot_t(rows, total).astype(BF16), columns)
        put_partial(both[:, :BLK], sino[...], mine, theirs, ray_dev)
        sums = both[:, BLK:]
        core = lax.rem(lax.axis_index("slab"), 2)
        top, low = sums[:total // 2], sums[total // 2:]
        mine[total // 2:total, :] = jnp.where(core == 0, top, low)
        theirs[total // 2:total, :] = jnp.where(core == 0, low, top)

    return kernel


def join_halves(mine, theirs):
    core = lax.rem(lax.axis_index("slab"), 2)
    mine, theirs = mine[...], theirs[...]
    return jnp.concatenate([jnp.where(core == 0, mine, theirs), jnp.where(core == 0, theirs, mine)], 0)


def next_forward(ray_dev):
    def kernel(proj, picks, places, volume, col_total, own, near, mid, far, sino, volume_out, weight_out, mine, theirs):
        weights = 1.0 / jnp.maximum(col_total[...], 1.0)
        weight_out[...] = weights
        updated = volume[...] + weights * ((own[...] + near[...]) + (mid[...] + far[...]))
        volume_out[...] = updated
        sums = forward_turned(proj, updated, picks[...], places[...])
        put_partial(sums, sino[...], mine, theirs, ray_dev)

    return kernel


def first_backward(proj, picks, places, mine, theirs, corr):
    corr[...] = backward(proj, join_halves(mine, theirs), picks[...], places[...])


def swap(x, axis, bit):
    size = lax.axis_size(axis)
    return lax.ppermute(x, axis, [(i, i ^ bit) for i in range(size)])


def over_slabs(mine, theirs, after=None):
    slabs = lax.axis_size("slab")
    x = mine + swap(theirs, "slab", 1)
    if after is not None:
        x, after = lax.optimization_barrier((x, after))
    bits = [1 << b for b in range(1, slabs.bit_length() - 1)]
    while bits:
        if len(bits) == 1:
            x, bits = x + swap(x, "slab", bits[0]), []
            continue
        first, second, bits = bits[0], bits[1], bits[2:]
        far = swap(x, "slab", first | second)
        x = (x + swap(x, "slab", first)) + (swap(x, "slab", second) + far)
    return x, after


def over_angles(x):
    angles = lax.axis_size("angle")
    for b in range(2, angles.bit_length() - 1):
        x = x + swap(x, "angle", 1 << b)
    return [x] + [swap(x, "angle", bit) for bit in ORDER]


def local(projector, block_vox, block_slot, send_ray, block_count, prior, sinogram):
    slabs = lax.axis_size("slab")
    capacity = send_ray.shape[1] // slabs
    ray_dev = sinogram.shape[0]
    vox_dev = prior.shape[0]
    blocks = projector.shape[0]
    half = slabs * ray_dev // 2
    params = pltpu.CompilerParams(vmem_limit_bytes=8 * 1024 * 1024)
    vmem = lambda rows, dtype=F32: pltpu.VMEM((rows, BLK), dtype)
    line = pltpu.VMEM((1, blocks), jnp.int32)
    arguments = (
        projector, block_vox.reshape(1, blocks), block_slot.reshape(1, blocks), send_ray,
        block_count.reshape(1, 1), prior, sinogram,
    )

    proj, vox, rows, volume, sino, mine, theirs = pl.pallas_call(
        first_forward(slabs, capacity, ray_dev),
        out_shape=(
            pltpu.VMEM(projector.shape, BF16), line, line, vmem(vox_dev), vmem(ray_dev),
            vmem(2 * half), vmem(2 * half),
        ),
        in_specs=[whole(pl.ANY)] * 7,
        out_specs=(whole(),) * 7,
        scratch_shapes=[
            line,
            pltpu.VMEM(send_ray.shape, jnp.int32),
            pltpu.VMEM((1, 1), jnp.int32),
            pltpu.SemaphoreType.DMA((2 * CHUNKS,)),
            pltpu.SemaphoreType.DMA((6,)),
        ],
        compiler_params=params,
        name="first_forward",
    )(*[x if x.size == 1 else pltpu.with_memory_space_constraint(x, pltpu.HBM) for x in arguments])
    from_rays, to_rays, from_vox, to_vox, col_total = pl.pallas_call(
        name_places,
        out_shape=(
            pltpu.VMEM((blocks, 2 * half), BF16), pltpu.VMEM((2 * half, blocks), BF16),
            pltpu.VMEM((blocks, vox_dev), BF16), pltpu.VMEM((vox_dev, blocks), BF16), vmem(vox_dev),
        ),
        in_specs=[whole()] * 3,
        out_specs=(whole(),) * 5,
        compiler_params=params,
        cost_estimate=pl.CostEstimate(flops=0, bytes_accessed=1 << 20, transcendentals=0),
        name="name_places",
    )(proj, rows, vox)
    turned = pl.pallas_call(
        turn_blocks,
        out_shape=pltpu.VMEM(projector.shape, BF16),
        in_specs=[whole()],
        out_specs=whole(),
        compiler_params=params,
        cost_estimate=pl.CostEstimate(flops=0, bytes_accessed=2 * projector.size * 2, transcendentals=0),
        name="turn_blocks",
    )(proj)
    sums, to_vox = over_slabs(mine, theirs, to_vox)
    row_weight = 1.0 / jnp.maximum(sums[half:], 1.0)
    weighted = (row_weight * sums[:half]).astype(BF16)
    angles = lax.axis_size("angle")
    for b in reversed(range(1, angles.bit_length() - 1)):
        col_total = col_total + swap(col_total, "angle", 1 << b)

    corr = pl.pallas_call(
        first_backward,
        out_shape=vmem(vox_dev),
        in_specs=[whole()] * 5,
        out_specs=whole(),
        compiler_params=params,
        name="first_backward",
    )(proj, from_rays, to_vox, weighted, swap(weighted, "slab", 1))
    col_total = col_total + swap(col_total, "angle", 1)

    volume, col_weight, mine, theirs = pl.pallas_call(
        next_forward(ray_dev),
        out_shape=(vmem(vox_dev), vmem(vox_dev), vmem(half), vmem(half)),
        in_specs=[whole()] * 10,
        out_specs=(whole(),) * 4,
        compiler_params=params,
        name="next_forward",
    )(turned, from_vox, to_rays, volume, col_total, *over_angles(corr), sino)
    residual, projector = over_slabs(mine, theirs, projector)
    count = blocks * 3 // 4
    fetched = [
        pl.pallas_call(
            fetch_blocks(low),
            out_shape=pltpu.VMEM((size,) + projector.shape[1:], BF16),
            in_specs=[whole(pl.ANY)],
            out_specs=whole(),
            scratch_shapes=[pltpu.SemaphoreType.DMA],
            compiler_params=params,
            cost_estimate=pl.CostEstimate(flops=0, bytes_accessed=size << 16, transcendentals=0),
            name="fetch_blocks",
        )(pltpu.with_memory_space_constraint(projector, pltpu.HBM))
        for low, size in ((0, count), (count, blocks - count))
    ]
    early, late = fetched
    residual, early = lax.optimization_barrier((residual, early))
    residual = row_weight * residual
    weighted = residual.astype(BF16)
    start = lax.div(lax.axis_index("slab"), 2) * ray_dev
    residual = lax.dynamic_slice_in_dim(residual, start, ray_dev)

    corr = pl.pallas_call(
        last_to_voxels,
        out_shape=vmem(vox_dev),
        in_specs=[whole()] * 6,
        out_specs=whole(),
        compiler_params=params,
        name="last_backward",
    )(early, late, from_rays, to_vox, weighted, swap(weighted, "slab", 1))
    volume = pl.pallas_call(
        last_update,
        out_shape=jax.ShapeDtypeStruct((vox_dev, BLK), F32),
        in_specs=[whole()] * 6,
        out_specs=whole(),
        compiler_params=params,
        name="last_update",
    )(volume, col_weight, *over_angles(corr))
    return volume, residual


def solution(mesh):
    return jax.shard_map(
        local,
        mesh=mesh,
        in_specs=(
            P(("slab", "angle"), None, None),
            P(("slab", "angle")),
            P(("slab", "angle")),
            P(("slab", "angle"), None),
            P(("slab", "angle")),
            P("slab", None),
            P(("slab", "angle"), None),
        ),
        out_specs=(P("slab", None), P(("slab", "angle"), None)),
        check_vma=False,
    )
```
